256 devices in a mesh: dp: 64 (over y_lo, z, x), tensor: 4 (over y_hi, core).
Axes of the slice: x: 4, y: 4 (y_hi: 2, y_lo: 2; y = y_hi * 2 + y_lo), z: 8, core: 2. Of those that a mesh axis runs over, the one named last changes fastest.
Arguments:
- img_feats: bfloat16 [16384, 1792], P('dp')
- txt_feats: bfloat16 [49152, 1024], P('dp')
- img_gain: float32 [1792], replicated, may hold values from 0.5 to 1.5
- txt_gain: float32 [1024], replicated, may hold values from 0.5 to 1.5
- img_weight: bfloat16 [1792, 1024], P(None, 'tensor')
- txt_weight: bfloat16 [1024, 1024], P(None, 'tensor')
- log_scale: float32 [1], replicated, may hold values from 2.5 to 2.9
- bias: float32 [1], replicated, may hold values from -10 to -8
- pair_perm: int32 [12288], replicated, may hold values from 0 to 12287, as said below
Outputs:
- loss: float32 [1], replicated
- img_weight_grad: float32 [1792, 1024], P(None, 'tensor')
- txt_weight_grad: float32 [1024, 1024], P(None, 'tensor')
- img_gain_grad: float32 [1792], replicated
- txt_gain_grad: float32 [1024], replicated
- scale_grad: float32 [1], replicated
- bias_grad: float32 [1], replicated
The draws below stay inside these ranges and needn't reach their ends.
Inputs may be any that keep to these rules, and one draw needn't show every extreme that they name: `pair_perm`: each text is the partner of exactly one image.
All inputs are finite; a program needn't handle non-finite values.
Results may differ from the reference program's by a relative error of at most 0.0046.
The reference program's roundings to bfloat16 on the way (of `grad_round`) count: a program that leaves them out, or rounds other values in their place, can miss the bound.
Values may be sent and summed in bfloat16 or wider, within the bound.
No kernel may reach another device: no remote copies, remote signals or barrier semaphores. Data moves between devices by JAX's collectives and lax.ppermute only.
A program may use at most 128 MiB of HBM per device.

```python
import math
import jax
import jax.numpy as jnp
from jax import lax

DI = 1792
DT = 1024
EMB = 1024
IMG_DEV = 256
TXT_DEV = 768
PAIRS = 12288
IMG_ROWS = 16384
TXT_ROWS = 49152
N_DP = 64


SIGNAL_PART = 0.3


SHARED_PART = 0.6


OWN_PART = 0.55


DIAGONAL = 2.0


def pairing(key):
    permuted = jax.random.permutation(jax.random.fold_in(key, 101), PAIRS).astype(jnp.int32)
    cluster_count = max(PAIRS // 8, 1)
    cluster = jax.random.randint(jax.random.fold_in(key, 102), (PAIRS,), 0, cluster_count).astype(jnp.int32)
    centres = jax.random.normal(jax.random.fold_in(key, 103), (cluster_count, EMB), jnp.float32)
    private = jax.random.normal(jax.random.fold_in(key, 104), (PAIRS, EMB), jnp.float32)
    shared = SIGNAL_PART * jnp.take(centres, cluster, axis=0) + SHARED_PART * private
    return (permuted, shared)


def diagonal_weight(fresh, fan_in):
    row_index = jnp.arange(fresh.shape[0], dtype=jnp.int32)[:, None]
    col_index = jnp.arange(EMB, dtype=jnp.int32)[None, :]
    return fresh * fan_in ** (-0.5) + jnp.where(row_index == col_index, DIAGONAL, 0.0).astype(jnp.float32)


def draw_pair_perm(key, part):
    permuted, shared = pairing(key)
    return permuted


def draw_img_feats(key, part):
    permuted, shared = pairing(key)
    key = jax.random.fold_in(key, 1)
    fresh_noise = jax.random.normal(key, (IMG_ROWS, DI), jnp.float32)
    row_index = jnp.arange(IMG_ROWS, dtype=jnp.int32)[:, None]
    col_index = jnp.arange(DI, dtype=jnp.int32)[None, :]
    inside = (row_index < PAIRS) & (col_index < EMB)
    placed = jnp.pad(shared, ((0, IMG_ROWS - PAIRS), (0, DI - EMB)))
    return (placed + jnp.where(inside, OWN_PART, 1.0).astype(jnp.float32) * fresh_noise).astype(jnp.bfloat16)


def draw_txt_feats(key, part):
    permuted, shared = pairing(key)
    key = jax.random.fold_in(key, 2)
    fresh_noise = jax.random.normal(key, (TXT_ROWS, DT), jnp.float32)
    inverse = jnp.zeros((PAIRS,), jnp.int32).at[permuted].set(jnp.arange(PAIRS, dtype=jnp.int32))
    partner_rows = jnp.take(shared, inverse, axis=0)
    first_text = TXT_ROWS - PAIRS
    row_index = jnp.arange(TXT_ROWS, dtype=jnp.int32)[:, None]
    col_index = jnp.arange(DT, dtype=jnp.int32)[None, :]
    inside = (row_index >= first_text) & (col_index < EMB)
    placed = jnp.pad(partner_rows, ((first_text, 0), (0, DT - EMB)))
    return (placed + jnp.where(inside, OWN_PART, 1.0).astype(jnp.float32) * fresh_noise).astype(jnp.bfloat16)


def draw_img_weight(key, part):
    key = jax.random.fold_in(key, 3)
    fresh = jax.random.normal(key, (DI, EMB), jnp.float32)
    return diagonal_weight(fresh, DI).astype(jnp.bfloat16)


def draw_txt_weight(key, part):
    key = jax.random.fold_in(key, 4)
    fresh = jax.random.normal(key, (DT, EMB), jnp.float32)
    return diagonal_weight(fresh, DT).astype(jnp.bfloat16)


def setup_inputs(seed: int = 0) -> dict:
    key_list = jax.random.split(jax.random.key(seed), 10)
    img_feats = draw_img_feats(jax.random.fold_in(key_list[9], 71), 0)
    txt_feats = draw_txt_feats(jax.random.fold_in(key_list[9], 71), 0)
    img_gain = jnp.clip(1.0 + 0.1 * jax.random.normal(key_list[2], (DI,), jnp.float32), 0.5, 1.5)
    txt_gain = jnp.clip(1.0 + 0.1 * jax.random.normal(key_list[3], (DT,), jnp.float32), 0.5, 1.5)
    img_weight = draw_img_weight(jax.random.fold_in(key_list[9], 71), 0)
    txt_weight = draw_txt_weight(jax.random.fold_in(key_list[9], 71), 0)
    log_scale = jnp.clip(jax.random.uniform(key_list[6], (1,), jnp.float32, 2.5, 2.9), 2.5, 2.9)
    bias = jnp.clip(jax.random.uniform(key_list[7], (1,), jnp.float32, -10.0, -8.0), -10.0, -8.0)
    pair_perm = draw_pair_perm(jax.random.fold_in(key_list[9], 71), 0)
    return {"img_feats": img_feats, "txt_feats": txt_feats, "img_gain": img_gain, "txt_gain": txt_gain, "img_weight": img_weight, "txt_weight": txt_weight, "log_scale": log_scale, "bias": bias, "pair_perm": pair_perm}


EPS = 1e-06

def normalize_rows(features, gain_vec):
    values = features.astype(jnp.float32)
    center = lax.optimization_barrier(jnp.mean(values, axis=1, keepdims=True))
    spread = lax.optimization_barrier(jnp.mean(values * values, axis=1, keepdims=True)) - center * center
    scaled = (values - center) * lax.rsqrt(spread + EPS)
    return ((scaled * gain_vec).astype(jnp.bfloat16), scaled)

def embed_rows(hidden, weight):
    project = jnp.dot(hidden, weight, preferred_element_type=jnp.float32)
    row_norms = jnp.sqrt(lax.optimization_barrier(jnp.sum(project * project, axis=1, keepdims=True)) + EPS)
    return ((project / row_norms).astype(jnp.bfloat16), row_norms)

def row_gradient(grad_full, embedded, row_norms):
    values = embedded.astype(jnp.float32)
    inner_dot = lax.optimization_barrier(jnp.sum(values * grad_full, axis=1, keepdims=True))
    return ((grad_full - values * inner_dot) / row_norms).astype(jnp.bfloat16)

def head_grads(hidden, scaled, weight, grad_round):
    weight_grad = lax.dot_general(hidden, grad_round, (((0,), (0,)), ((), ())), preferred_element_type=jnp.float32)
    hidden_grad = lax.dot_general(grad_round, weight, (((1,), (1,)), ((), ())), preferred_element_type=jnp.float32)
    return (weight_grad, lax.optimization_barrier(jnp.sum(hidden_grad * scaled, axis=0)))

def reference(img_feats, txt_feats, img_gain, txt_gain, img_weight, txt_weight, log_scale, bias, pair_perm):
    image_devices = N_DP - N_DP // 4
    images = img_feats[:image_devices * IMG_DEV]
    texts = txt_feats[image_devices * TXT_DEV:]
    image_hidden, image_hat = normalize_rows(images, img_gain)
    text_hidden, text_hat = normalize_rows(texts, txt_gain)
    image_emb, image_norm = embed_rows(image_hidden, img_weight)
    text_emb, text_norm = embed_rows(text_hidden, txt_weight)
    logit_scale = jnp.exp(log_scale[0])
    logit_bias = bias[0]
    block_rows = math.gcd(PAIRS, 512)
    columns = jnp.arange(PAIRS, dtype=jnp.int32)

    def one_block(state, offset):
        loss_sum, scale_sum, bias_sum, text_acc = state
        row_embed = lax.dynamic_slice_in_dim(image_emb, offset, block_rows, 0)
        partner = lax.dynamic_slice_in_dim(pair_perm, offset, block_rows, 0)
        similar = lax.dot_general(row_embed, text_emb, (((1,), (1,)), ((), ())), preferred_element_type=jnp.float32)
        logits = logit_scale * similar + logit_bias
        labels = jnp.where(partner[:, None] == columns[None, :], 1.0, -1.0).astype(jnp.float32)
        grad_tile = -labels * jax.nn.sigmoid(-labels * logits)
        loss_sum = loss_sum - jnp.sum(jax.nn.log_sigmoid(labels * logits))
        scale_sum = scale_sum + jnp.sum(grad_tile * similar)
        bias_sum = bias_sum + jnp.sum(grad_tile)
        grad_round = grad_tile.astype(jnp.bfloat16)
        text_acc = text_acc + lax.dot_general(grad_round, row_embed, (((0,), (0,)), ((), ())), preferred_element_type=jnp.float32)
        grad_rows = logit_scale * jnp.dot(grad_round, text_emb, preferred_element_type=jnp.float32)
        return ((loss_sum, scale_sum, bias_sum, text_acc), grad_rows)
    initial = (jnp.zeros((), jnp.float32), jnp.zeros((), jnp.float32), jnp.zeros((), jnp.float32), jnp.zeros((PAIRS, EMB), jnp.float32))
    offsets = jnp.arange(PAIRS // block_rows, dtype=jnp.int32) * block_rows
    (loss_sum, scale_sum, bias_sum, text_acc), grad_rows = lax.scan(one_block, initial, offsets)
    image_dz = grad_rows.reshape(PAIRS, EMB)
    text_dz = logit_scale * text_acc
    image_du = row_gradient(image_dz, image_emb, image_norm)
    text_du = row_gradient(text_dz, text_emb, text_norm)
    img_weight_grad, img_gain_grad = head_grads(image_hidden, image_hat, img_weight, image_du)
    txt_weight_grad, txt_gain_grad = head_grads(text_hidden, text_hat, txt_weight, text_du)
    loss = jnp.reshape(loss_sum / PAIRS, (1,))
    scale_grad = jnp.reshape(logit_scale * scale_sum, (1,))
    bias_grad = jnp.reshape(bias_sum, (1,))
    return (loss, img_weight_grad, txt_weight_grad, img_gain_grad, txt_gain_grad, scale_grad, bias_grad)
```

```python
import jax
import jax.numpy as jnp
from jax import lax
from jax.experimental import pallas as pl
from jax.experimental.pallas import tpu as pltpu
from jax.sharding import Mesh, PartitionSpec as P

EPS = 1e-06
F32 = jnp.float32
BF16 = jnp.bfloat16
Z = 8
TEXT_Z = 4
DP = ("yl", "z", "x")
STEPS = 4


def hidden_rows(features, gain_vec):
    values = features.astype(F32)
    center = jnp.mean(values, axis=1, keepdims=True)
    spread = jnp.mean(values * values, axis=1, keepdims=True) - center * center
    scaled = (values - center) * lax.rsqrt(spread + EPS)
    return (scaled * gain_vec).astype(BF16)


def swap(value, axis):
    return lax.ppermute(value, axis, [(0, 1), (1, 0)])


def exchange(value, axes):
    return lax.all_to_all(value, axes, split_axis=0, concat_axis=0, tiled=True)


def split3(value):
    high = value.astype(BF16)
    rest = value - high.astype(F32)
    middle = rest.astype(BF16)
    return high, middle, (rest - middle.astype(F32)).astype(BF16)


def tile_kernel(
    factors, valid, partner, columns, emb_i, emb_t, out_i, out_t, out_s, acc, sums
):
    step = pl.program_id(0)
    scale, shift = factors[0], factors[1]

    @pl.when(step == 0)
    def _():
        acc[...] = jnp.zeros_like(acc)
        sums[...] = jnp.zeros_like(sums)

    @pl.when(valid[step] == 0)
    def _():
        out_i[...] = jnp.zeros_like(out_i)

    @pl.when(valid[step] != 0)
    def _():
        rows = jnp.concatenate(
            [
                jnp.concatenate([emb_i[0], emb_i[1]], axis=1),
                jnp.concatenate([emb_i[2], emb_i[3]], axis=1),
            ],
            axis=0,
        )
        texts = emb_t[...]
        similar = lax.dot_general(rows, texts, (((1,), (1,)), ((), ())), preferred_element_type=F32)
        logits = scale * similar + shift
        pair = partner[...] == columns[...]
        signed = jnp.where(pair, -logits, logits)
        small = jnp.exp(-jnp.abs(signed))
        total = 1.0 + small
        inverse = 1.0 / total
        sigmoid = jnp.where(signed >= 0, inverse, small * inverse)
        soft = jnp.maximum(signed, 0.0) + jnp.log(total) + (small - (total - 1.0)) * inverse
        grad = jnp.where(pair, -sigmoid, sigmoid)
        sums[0:1] += jnp.sum(soft, axis=0, keepdims=True)
        sums[1:2] += jnp.sum(grad * similar, axis=0, keepdims=True)
        sums[2:3] += jnp.sum(grad, axis=0, keepdims=True)
        rounded = grad.astype(BF16)
        acc[...] += lax.dot_general(rounded, rows, (((0,), (0,)), ((), ())), preferred_element_type=F32)
        grad_rows = jnp.dot(rounded, texts, preferred_element_type=F32)
        wide = rows.astype(F32)
        inner = jnp.sum(wide * grad_rows, axis=1, keepdims=True)
        result = (scale * (grad_rows - wide * inner)).astype(BF16)
        half = result.shape[1] // 2
        high = result.shape[0] // 2
        out_i[0] = result[:high, :half]
        out_i[1] = result[:high, half:]
        out_i[2] = result[high:, :half]
        out_i[3] = result[high:, half:]

    @pl.when(step == STEPS - 1)
    def _():
        texts = emb_t[...].astype(F32)
        grads = acc[...]
        inner = jnp.sum(texts * grads, axis=1, keepdims=True)
        out_t[...] = (scale * (grads - texts * inner)).astype(BF16)
        out_s[...] = jnp.broadcast_to(jnp.sum(sums[...], axis=1, keepdims=True), out_s.shape)


def tile_grads(factors, valid, partner, columns, emb_i, emb_t):
    slabs, high, half = emb_i.shape
    block = slabs // STEPS
    count, width = emb_t.shape
    return pl.pallas_call(
        tile_kernel,
        grid=(STEPS,),
        in_specs=[
            pl.BlockSpec(memory_space=pltpu.SMEM),
            pl.BlockSpec(memory_space=pltpu.SMEM),
            pl.BlockSpec((partner.shape[0] // STEPS, 1), lambda i: (i, 0)),
            pl.BlockSpec((1, count), lambda i: (0, 0)),
            pl.BlockSpec((block, high, half), lambda i: (i, 0, 0)),
            pl.BlockSpec((count, width), lambda i: (0, 0)),
        ],
        out_specs=[
            pl.BlockSpec((block, high, half), lambda i: (i, 0, 0)),
            pl.BlockSpec((count, width), lambda i: (0, 0)),
            pl.BlockSpec((8, 128), lambda i: (0, 0)),
        ],
        out_shape=[
            jax.ShapeDtypeStruct(emb_i.shape, BF16),
            jax.ShapeDtypeStruct(emb_t.shape, BF16),
            jax.ShapeDtypeStruct((8, 128), F32),
        ],
        scratch_shapes=[pltpu.VMEM((count, width), F32), pltpu.VMEM((8, count), F32)],
        compiler_params=pltpu.CompilerParams(vmem_limit_bytes=40 * 1024 * 1024),
    )(factors, valid, partner, columns, emb_i, emb_t)


def half_place(half, j):
    return TEXT_Z + j if half else TEXT_Z - 1 - j


def turn(k):
    return [
        (half_place(half, j), half_place(half, (j + k) % TEXT_Z))
        for half in range(2)
        for j in range(TEXT_Z)
    ]


def local(
    img_feats, txt_feats, img_gain, txt_gain, img_weight, txt_weight, log_scale, bias, pair_perm
):
    yl, z, x = lax.axis_index("yl"), lax.axis_index("z"), lax.axis_index("x")
    yh, core = lax.axis_index("yh"), lax.axis_index("co")
    pair_count = pair_perm.shape[0]
    img_count, txt_count = img_feats.shape[0], txt_feats.shape[0]
    is_text = (yl == 1) & (z >= TEXT_Z)
    near = jnp.where(z >= TEXT_Z, z - TEXT_Z, TEXT_Z - 1 - z)

    text_hidden = hidden_rows(txt_feats, txt_gain)
    image_hidden = hidden_rows(img_feats, img_gain)
    text_proj = jnp.dot(text_hidden, txt_weight, preferred_element_type=F32)
    image_proj = jnp.dot(image_hidden, img_weight, preferred_element_type=F32)
    squares = jnp.concatenate(
        [jnp.sum(text_proj * text_proj, axis=1), jnp.sum(image_proj * image_proj, axis=1)]
    )
    squares = squares + swap(squares, "co")
    squares = squares + swap(squares, "yh")
    norms = jnp.sqrt(squares + EPS)[:, None]
    text_norm, image_norm = norms[:txt_count], norms[txt_count:]
    text_emb = (text_proj / text_norm).astype(BF16)
    image_emb = (image_proj / image_norm).astype(BF16)

    image_half = lax.all_to_all(image_emb, "co", split_axis=0, concat_axis=1, tiled=True)
    image_all = lax.all_gather(image_half, ("yl", "x", "yh"), axis=0, tiled=False)

    piece = txt_count // 8
    text_half = lax.all_to_all(text_emb, "co", split_axis=0, concat_axis=1, tiled=True)
    width = text_half.shape[1]
    text_half = text_half.reshape(4, piece, width)

    def part(q):
        return lax.dynamic_index_in_dim(text_half, q, 0, keepdims=False)

    def y_index(pairs):
        return [(a[0] * 2 + a[1], b[0] * 2 + b[1]) for a, b in pairs]

    across = y_index([((1, 0), (1, 1)), ((1, 1), (1, 0))])
    straight = y_index([((1, 0), (0, 0)), ((1, 1), (0, 1))])
    diagonal = y_index([((1, 0), (0, 1)), ((1, 1), (0, 0))])
    ys = ("yl", "yh")
    got_across = lax.ppermute(part(2 + (1 - yh)), ys, across)
    got_straight = lax.ppermute(part(yh), ys, straight)
    got_diagonal = lax.ppermute(part(1 - yh), ys, diagonal)
    mine = jnp.where(yl == 1, part(2 + yh), got_straight)
    other = jnp.where(yl == 1, got_across, got_diagonal)
    chunk = jnp.where(
        yh == 0,
        jnp.concatenate([mine, other], axis=1),
        jnp.concatenate([other, mine], axis=1),
    )
    mirror = [(a, Z - 1 - a) for a in range(TEXT_Z, Z)]
    got_mirror = lax.ppermute(chunk, "z", mirror)
    chunk = jnp.where(z >= TEXT_Z, chunk, got_mirror)
    chunks = jnp.stack([chunk] + [lax.ppermute(chunk, "z", turn(k)) for k in range(1, TEXT_Z)])
    text_tile = lax.all_gather(chunks, "co", axis=0, tiled=False)
    text_tile = text_tile.reshape(2 * TEXT_Z * piece, 2 * width)

    quarter = yl * 2 + yh
    order = jnp.arange(TEXT_Z, dtype=jnp.int32)
    group = jnp.mod(near - order + TEXT_Z, TEXT_Z) * 4 + x
    columns = (
        group[None, :, None] * txt_count
        + jnp.arange(2, dtype=jnp.int32)[:, None, None] * (4 * piece)
        + quarter * piece
        + jnp.arange(piece, dtype=jnp.int32)[None, None, :]
    ).reshape(1, -1)
    padded = jnp.concatenate(
        [pair_perm, jnp.full((16 * img_count,), -1, jnp.int32)]
    ).reshape(2, Z, 4, 2, img_count // 2)
    partner = lax.dynamic_index_in_dim(
        lax.dynamic_index_in_dim(padded, z, 1, keepdims=False), core, 2, keepdims=False
    ).reshape(-1, 1)
    valid = jnp.concatenate(
        [jnp.ones((2,), jnp.int32), jnp.full((2,), 1, jnp.int32) * (z < TEXT_Z).astype(jnp.int32)]
    )
    logit_scale = jnp.exp(log_scale[0])
    factors = jnp.stack([logit_scale, bias[0]])
    image_part, text_part, part_sums = tile_grads(
        factors,
        valid,
        partner,
        columns,
        image_all.reshape(16, img_count // 2, width),
        text_tile,
    )

    image_sum = jnp.sum(
        exchange(image_part, ("yl", "x", "yh")).astype(F32), axis=0
    )
    half_norm = lax.dynamic_slice_in_dim(image_norm, core * (img_count // 2), img_count // 2, 0)
    image_du = lax.all_to_all(
        (image_sum / half_norm).astype(BF16), "co", split_axis=1, concat_axis=0, tiled=True
    )

    text_part = text_part.reshape(2, TEXT_Z, piece, 2 * width)
    kept = lax.dynamic_index_in_dim(text_part, core, 0, keepdims=False)
    sent = lax.dynamic_index_in_dim(text_part, 1 - core, 0, keepdims=False)
    both = kept.astype(F32) + swap(sent, "co").astype(F32)
    rounded = both.astype(BF16)
    text_sum = both[0]
    for k in range(1, TEXT_Z):
        text_sum = text_sum + lax.ppermute(rounded[k], "z", turn(TEXT_Z - k)).astype(F32)
    text_sum = text_sum + lax.ppermute(
        text_sum.astype(BF16), "z", [(b, a) for a, b in mirror]
    ).astype(F32)
    text_sum = text_sum.astype(BF16)
    text_low, text_high = text_sum[:, :width], text_sum[:, width:]
    same = jnp.where(yh == 0, text_low, text_high)
    cross = jnp.where(yh == 0, text_high, text_low)

    def back(pairs):
        return [(b, a) for a, b in pairs]

    back_across = lax.ppermute(cross, ys, back(across))
    back_straight = lax.ppermute(same, ys, back(straight))
    back_diagonal = lax.ppermute(cross, ys, back(diagonal))
    text_rows = jnp.where(
        yh == 0,
        jnp.concatenate([back_straight, back_diagonal, same, back_across], axis=0),
        jnp.concatenate([back_diagonal, back_straight, back_across, same], axis=0),
    )
    text_back = lax.all_to_all(text_rows, "co", split_axis=1, concat_axis=0, tiled=True)
    text_du = jnp.where(is_text, text_back.astype(F32) / text_norm, 0.0).astype(BF16)

    transposed = (((0,), (0,)), ((), ()))
    weight_part = jnp.concatenate(
        [
            lax.dot_general(image_hidden, image_du, transposed, preferred_element_type=F32),
            lax.dot_general(text_hidden, text_du, transposed, preferred_element_type=F32),
        ],
        axis=0,
    )
    total_rows, cols = weight_part.shape
    share = total_rows // 64
    loss_parts = part_sums[:3, 0]

    def small_rows(values, lead):
        parts = jnp.stack(split3(values), axis=0)
        parts = jnp.pad(parts, ((0, 1), (0, cols - values.shape[0])))
        return jnp.broadcast_to(parts, (*lead, 4, cols))

    def join(rows):
        return rows[0] + rows[1] + rows[2]

    sent = jnp.concatenate(
        [weight_part.astype(BF16).reshape(4, 16, share, cols), small_rows(loss_parts, (4, 16))],
        axis=2,
    )
    reduced = jnp.sum(exchange(sent, "x").astype(F32), axis=0)
    loss_parts = join(reduced[0, share:])[:3]
    sent = jnp.concatenate(
        [reduced[:, :share].astype(BF16), small_rows(loss_parts, (16,))], axis=1
    )
    reduced = jnp.sum(exchange(sent, ("yl", "z")).astype(F32), axis=0)
    loss_parts = join(reduced[share:])[:3]
    weight_sum = reduced[:share]
    own = (x * 16 + yl * Z + z) * share
    own_weight = lax.dynamic_slice_in_dim(
        jnp.concatenate([img_weight, txt_weight], axis=0), own, share, 0
    )
    own_gain = lax.dynamic_slice_in_dim(jnp.concatenate([img_gain, txt_gain]), own, share, 0)
    gain_sum = jnp.sum(weight_sum * own_weight.astype(F32), axis=1) / own_gain
    small = jnp.concatenate([gain_sum, loss_parts])
    small = small + swap(small, "co")
    small = small + swap(small, "yh")
    gain_sum, loss_parts = small[:share], small[share:]
    ready = jnp.concatenate([weight_sum.astype(BF16), small_rows(gain_sum, ())], axis=0)
    gathered = exchange(jnp.broadcast_to(ready, (16, *ready.shape)), ("yl", "z"))
    gathered = exchange(jnp.broadcast_to(gathered, (4, *gathered.shape)), "x").astype(F32)
    weight_grad = gathered[:, :, :share].reshape(total_rows, cols)
    gain_grad = jnp.sum(gathered[:, :, share:, :share], axis=2).reshape(total_rows)
    split = img_weight.shape[0]
    return (
        loss_parts[0:1] / pair_count,
        weight_grad[:split],
        weight_grad[split:],
        gain_grad[:split],
        gain_grad[split:],
        loss_parts[1:2] * logit_scale,
        loss_parts[2:3],
    )


def solution(mesh):
    inner = Mesh(mesh.devices.reshape(2, Z, 4, 2, 2), ("yl", "z", "x", "yh", "co"))
    tensor = ("yh", "co")
    return jax.shard_map(
        local,
        mesh=inner,
        in_specs=(
            P(DP, None),
            P(DP, None),
            P(),
            P(),
            P(None, tensor),
            P(None, tensor),
            P(),
            P(),
            P(),
        ),
        out_specs=(P(), P(None, tensor), P(None, tensor), P(), P(), P(), P()),
        check_vma=False,
    )
```

```python
import jax
import jax.numpy as jnp
from jax import lax
from jax.experimental import pallas as pl
from jax.experimental.pallas import tpu as pltpu
from jax.sharding import Mesh, PartitionSpec as P

EPS = 1e-06
F32 = jnp.float32
BF16 = jnp.bfloat16
Z = 8
TEXT_Z = 4
DP = ("yl", "z", "x")
STEPS = 4


def hidden_rows(features, gain_vec):
    values = features.astype(F32)
    center = jnp.mean(values, axis=1, keepdims=True)
    spread = jnp.mean(values * values, axis=1, keepdims=True) - center * center
    scaled = (values - center) * lax.rsqrt(spread + EPS)
    return (scaled * gain_vec).astype(BF16)


def swap(value, axis):
    return lax.ppermute(value, axis, [(0, 1), (1, 0)])


def exchange(value, axes):
    return lax.all_to_all(value, axes, split_axis=0, concat_axis=0, tiled=True)


def split3(value):
    high = value.astype(BF16)
    rest = value - high.astype(F32)
    middle = rest.astype(BF16)
    return high, middle, (rest - middle.astype(F32)).astype(BF16)


def tile_kernel(
    factors, partner, columns, emb_i, emb_t, out_i, out_t, out_s, acc, sums
):
    step = pl.program_id(0)
    scale, shift = factors[0], factors[1]

    @pl.when(step == 0)
    def _():
        acc[...] = jnp.zeros_like(acc)
        sums[...] = jnp.zeros_like(sums)

    rows = jnp.concatenate(
        [
            jnp.concatenate([emb_i[0], emb_i[1]], axis=1),
            jnp.concatenate([emb_i[2], emb_i[3]], axis=1),
        ],
        axis=0,
    )
    texts = emb_t[...]
    high = emb_i.shape[1]
    half = emb_i.shape[2]
    place = lax.broadcasted_iota(jnp.int32, (2 * high, 1), 0)
    weight = jnp.where(place < high, factors[2], factors[3])
    similar = lax.dot_general(rows, texts, (((1,), (1,)), ((), ())), preferred_element_type=F32)
    logits = scale * similar + shift
    pair = partner[...] == columns[...]
    signed = jnp.where(pair, -logits, logits)
    small = jnp.exp(-jnp.abs(signed))
    total = 1.0 + small
    inverse = 1.0 / total
    sigmoid = jnp.where(signed >= 0, inverse, small * inverse)
    soft = jnp.maximum(signed, 0.0) + jnp.log(total) + (small - (total - 1.0)) * inverse
    grad = jnp.where(pair, -sigmoid, sigmoid) * weight
    sums[0:1] += jnp.sum(soft * weight, axis=0, keepdims=True)
    sums[1:2] += jnp.sum(grad * similar, axis=0, keepdims=True)
    sums[2:3] += jnp.sum(grad, axis=0, keepdims=True)
    rounded = grad.astype(BF16)
    acc[...] += lax.dot_general(rounded, rows, (((0,), (0,)), ((), ())), preferred_element_type=F32)
    grad_rows = jnp.dot(rounded, texts, preferred_element_type=F32)
    wide = rows.astype(F32)
    inner = jnp.sum(wide * grad_rows, axis=1, keepdims=True)
    result = (scale * (grad_rows - wide * inner)).astype(BF16)
    out_i[0] = result[:high, :half]
    out_i[1] = result[:high, half:]
    out_i[2] = result[high:, :half]
    out_i[3] = result[high:, half:]

    @pl.when(step == STEPS - 1)
    def _():
        texts = emb_t[...].astype(F32)
        grads = acc[...]
        inner = jnp.sum(texts * grads, axis=1, keepdims=True)
        out_t[...] = (scale * (grads - texts * inner)).astype(BF16)
        out_s[...] = jnp.broadcast_to(jnp.sum(sums[...], axis=1, keepdims=True), out_s.shape)


def tile_grads(factors, partner, columns, emb_i, emb_t):
    slabs, high, half = emb_i.shape
    block = slabs // STEPS
    count, width = emb_t.shape
    return pl.pallas_call(
        tile_kernel,
        grid=(STEPS,),
        in_specs=[
            pl.BlockSpec(memory_space=pltpu.SMEM),
            pl.BlockSpec((partner.shape[0] // STEPS, 1), lambda i: (i, 0)),
            pl.BlockSpec((1, count), lambda i: (0, 0)),
            pl.BlockSpec((block, high, half), lambda i: (i, 0, 0)),
            pl.BlockSpec((count, width), lambda i: (0, 0)),
        ],
        out_specs=[
            pl.BlockSpec((block, high, half), lambda i: (i, 0, 0)),
            pl.BlockSpec((count, width), lambda i: (0, 0)),
            pl.BlockSpec((8, 128), lambda i: (0, 0)),
        ],
        out_shape=[
            jax.ShapeDtypeStruct(emb_i.shape, BF16),
            jax.ShapeDtypeStruct(emb_t.shape, BF16),
            jax.ShapeDtypeStruct((8, 128), F32),
        ],
        scratch_shapes=[pltpu.VMEM((count, width), F32), pltpu.VMEM((8, count), F32)],
        compiler_params=pltpu.CompilerParams(vmem_limit_bytes=40 * 1024 * 1024),
    )(factors, partner, columns, emb_i, emb_t)


def half_place(half, j):
    return TEXT_Z + j if half else TEXT_Z - 1 - j


def turn(k):
    return [
        (half_place(half, j), half_place(half, (j + k) % TEXT_Z))
        for half in range(2)
        for j in range(TEXT_Z)
    ]


def finish_kernel(places, first, second, third, fourth, out_i, out_t, out_g, rows):
    image_rows = rows.shape[0] // 16
    text_rows = out_t.shape[0] // 64
    padded = first.shape[1] - text_rows
    for k, piece in enumerate((first, second, third, fourth)):
        place = places[k]
        for s in range(16):
            values = piece[s].astype(F32)
            rows[s * image_rows : (s + 1) * image_rows] = values[:image_rows]
            start = pl.multiple_of(place * (16 * text_rows) + s * text_rows, 8)
            out_t[pl.ds(start, text_rows)] = values[padded:]
            tail = values[image_rows:padded]
            out_g[place, s : s + 1] = tail[0:1] + tail[1:2] + tail[2:3]
        start = pl.multiple_of(place * (16 * image_rows), 8)
        out_i[pl.ds(start, 16 * image_rows)] = rows[...]


def finish(places, pieces, image_total, text_total):
    cols = pieces[0].shape[2]
    whole = pl.BlockSpec(memory_space=pltpu.VMEM)
    return pl.pallas_call(
        finish_kernel,
        in_specs=[pl.BlockSpec(memory_space=pltpu.SMEM)] + [whole] * 4,
        out_specs=[whole] * 3,
        out_shape=[
            jax.ShapeDtypeStruct((image_total, cols), F32),
            jax.ShapeDtypeStruct((text_total, cols), F32),
            jax.ShapeDtypeStruct((4, 16, cols), F32),
        ],
        scratch_shapes=[pltpu.VMEM((image_total // 4, cols), F32)],
        compiler_params=pltpu.CompilerParams(vmem_limit_bytes=24 * 1024 * 1024),
    )(places, *pieces)


def ring(k):
    return [(i, (i + k) % 4) for i in range(4)]


def y_move(value, k):
    return lax.ppermute(value, ("yl", "yh"), [(i, i ^ k) for i in range(4)])


def pick(value, index, axis=0):
    return lax.dynamic_index_in_dim(value, index, axis, keepdims=False)


def local(
    img_feats, txt_feats, img_gain, txt_gain, img_weight, txt_weight, log_scale, bias, pair_perm
):
    yl, z, x = lax.axis_index("yl"), lax.axis_index("z"), lax.axis_index("x")
    yh, core = lax.axis_index("yh"), lax.axis_index("co")
    pair_count = pair_perm.shape[0]
    img_count, txt_count = img_feats.shape[0], txt_feats.shape[0]
    img_half, txt_half = img_count // 2, txt_count // 2
    piece = txt_half // 4
    is_text = (yl == 1) & (z >= TEXT_Z)
    near = jnp.where(z >= TEXT_Z, z - TEXT_Z, TEXT_Z - 1 - z)
    sources = [jnp.mod(x - k + 4, 4) for k in range(4)]
    targets = [jnp.mod(x + k, 4) for k in range(4)]

    text_hidden = hidden_rows(txt_feats, txt_gain)
    image_hidden = hidden_rows(img_feats, img_gain)
    text_proj = jnp.dot(text_hidden, txt_weight, preferred_element_type=F32)
    image_proj = jnp.dot(image_hidden, img_weight, preferred_element_type=F32)
    squares = jnp.concatenate(
        [jnp.sum(text_proj * text_proj, axis=1), jnp.sum(image_proj * image_proj, axis=1)]
    )
    squares = squares + swap(squares, "co")
    squares = squares + swap(squares, "yh")
    norms = jnp.sqrt(squares + EPS)[:, None]
    text_norm, image_norm = norms[:txt_count], norms[txt_count:]
    text_emb = (text_proj / text_norm).astype(BF16)
    image_emb = (image_proj / image_norm).astype(BF16)

    def halves(index):
        return jnp.concatenate(
            [
                lax.dynamic_slice_in_dim(image_emb, index * img_half, img_half, 0),
                lax.dynamic_slice_in_dim(text_emb, index * txt_half, txt_half, 0),
            ],
            axis=0,
        )

    kept = halves(core)
    taken = swap(halves(1 - core), "co")
    both = jnp.where(
        core == 0,
        jnp.concatenate([kept, taken], axis=1),
        jnp.concatenate([taken, kept], axis=1),
    )
    width = both.shape[1]
    image_own = both[:img_half]
    text_own = both[img_half:].reshape(4, piece, width)

    got = []
    for k in range(1, 4):
        target = jnp.bitwise_xor(yl * 2 + yh, k)
        got.append(y_move(jnp.concatenate([image_own, pick(text_own, target)], axis=0), k))
    slabs = jnp.stack([image_own] + [g[:img_half] for g in got])
    mine = jnp.where(yl == 1, pick(text_own, yl * 2 + yh), got[1][img_half:])
    other = jnp.where(yl == 1, got[0][img_half:], got[2][img_half:])
    chunk = jnp.concatenate([mine, other], axis=1)
    mirror = [(a, Z - 1 - a) for a in range(TEXT_Z, Z)]
    chunk = jnp.where(z >= TEXT_Z, chunk, lax.ppermute(chunk, "z", mirror))
    image_all = jnp.concatenate([slabs] + [lax.ppermute(slabs, "x", ring(k)) for k in range(1, 4)])
    chunks = jnp.stack([chunk] + [lax.ppermute(chunk, "z", turn(k)) for k in range(1, TEXT_Z)])
    text_tile = jnp.stack([chunks, swap(chunks, "co")])
    text_tile = text_tile.reshape(2 * TEXT_Z * piece, 2 * width)

    quarter = yl * 2 + yh
    order = jnp.arange(TEXT_Z, dtype=jnp.int32)
    group = jnp.mod(near - order + TEXT_Z, TEXT_Z) * 4 + x
    columns = (
        group[None, :, None] * txt_count
        + jnp.mod(core + jnp.arange(2, dtype=jnp.int32), 2)[:, None, None] * txt_half
        + quarter * piece
        + jnp.arange(piece, dtype=jnp.int32)[None, None, :]
    ).reshape(1, -1)
    padded = jnp.concatenate([pair_perm, jnp.full((16 * img_count,), -1, jnp.int32)])
    padded = pick(pick(padded.reshape(2, Z, 4, 2, img_half), z, 1), core, 2)
    padded = jnp.where(yl == 0, padded, padded[::-1])
    partner = jnp.stack([pick(padded, source, 1) for source in sources]).reshape(-1, 1)
    logit_scale = jnp.exp(log_scale[0])
    weights = [
        jnp.where((side == 1) & (z >= TEXT_Z), 0.0, 1.0).astype(F32) for side in (yl, 1 - yl)
    ]
    factors = jnp.stack([logit_scale, bias[0], *weights])

    share_cols = image_hidden.shape[1] // 4
    parts = jnp.stack(
        [image_hidden[:, i * share_cols : (i + 1) * share_cols] for i in range(4)]
    )
    hidden_x = jnp.concatenate(
        [pick(parts, x)]
        + [lax.ppermute(pick(parts, targets[k]), "x", ring(k)) for k in range(1, 4)]
    )

    image_part, text_part, part_sums = tile_grads(factors, partner, columns, image_all, text_tile)

    image_part = image_part.reshape(4, 4, img_half, width)
    image_sum = image_part[0].astype(F32)
    for k in range(1, 4):
        image_sum = image_sum + lax.ppermute(image_part[k], "x", ring(-k)).astype(F32)

    text_part = text_part.reshape(2, TEXT_Z, piece, 2 * width)
    both = text_part[0].astype(F32) + swap(text_part[1], "co").astype(F32)
    rounded = both.astype(BF16)
    text_sum = both[0]
    for k in range(1, TEXT_Z):
        text_sum = text_sum + lax.ppermute(rounded[k], "z", turn(TEXT_Z - k)).astype(F32)
    text_sum = text_sum + lax.ppermute(
        text_sum.astype(BF16), "z", [(b, a) for a, b in mirror]
    ).astype(F32)
    text_sum = text_sum.astype(BF16)
    same, cross = text_sum[:, :width], text_sum[:, width:]
    image_round = image_sum.astype(BF16)
    got = [
        y_move(jnp.concatenate([image_round[k], cross if k & 1 else same], axis=0), k)
        for k in range(1, 4)
    ]
    image_sum = image_sum[0]
    for g in got:
        image_sum = image_sum + g[:img_half].astype(F32)
    across, straight, diagonal = [g[img_half:] for g in got]
    text_rows = jnp.where(
        yh == 0,
        jnp.concatenate([straight, diagonal, same, across], axis=0),
        jnp.concatenate([diagonal, straight, across, same], axis=0),
    )
    image_rows = image_sum / lax.dynamic_slice_in_dim(image_norm, core * img_half, img_half, 0)
    text_rows = text_rows.astype(F32) / lax.dynamic_slice_in_dim(
        text_norm, core * txt_half, txt_half, 0
    )
    text_rows = jnp.where(is_text, text_rows, 0.0)
    both = jnp.concatenate([image_rows.astype(BF16), text_rows.astype(BF16)], axis=0)
    cols = width // 2
    kept = lax.dynamic_slice_in_dim(both, core * cols, cols, 1)
    taken = swap(lax.dynamic_slice_in_dim(both, (1 - core) * cols, cols, 1), "co")
    first = jnp.where(core == 0, kept, taken)
    second = jnp.where(core == 0, taken, kept)
    image_du = jnp.concatenate([first[:img_half], second[:img_half]], axis=0)
    text_du = jnp.concatenate([first[img_half:], second[img_half:]], axis=0)

    transposed = (((0,), (0,)), ((), ()))
    text_weight = lax.dot_general(text_hidden, text_du, transposed, preferred_element_type=F32)
    text_share = text_weight.shape[0] // 4
    text_weight = text_weight.reshape(4, text_share, cols)
    loss_parts = part_sums[:3, 0]

    def small_rows(values, count):
        rows = jnp.stack(split3(values), axis=0)
        return jnp.pad(rows, ((0, count - 3), (0, cols - values.shape[0])))

    def join(rows):
        return rows[0] + rows[1] + rows[2]

    tail = small_rows(loss_parts, 16)
    got = [
        lax.ppermute(
            jnp.concatenate([image_du, pick(text_weight, targets[k]).astype(BF16), tail], axis=0),
            "x",
            ring(k),
        )
        for k in range(1, 4)
    ]
    du_x = jnp.concatenate([image_du] + [g[:img_count] for g in got], axis=0)
    text_weight = pick(text_weight, x)
    for g in got:
        text_weight = text_weight + g[img_count : img_count + text_share].astype(F32)
        loss_parts = loss_parts + join(g[img_count + text_share :].astype(F32))[:3]
    image_weight = lax.dot_general(hidden_x, du_x, transposed, preferred_element_type=F32)

    img_share, txt_share = share_cols // 16, text_share // 16
    slot = 32
    block = jnp.concatenate(
        [
            image_weight.astype(BF16).reshape(16, img_share, cols),
            jnp.broadcast_to(
                small_rows(loss_parts, slot - img_share), (16, slot - img_share, cols)
            ),
            text_weight.astype(BF16).reshape(16, txt_share, cols),
        ],
        axis=1,
    )
    reduced = jnp.sum(exchange(block, ("yl", "z")).astype(F32), axis=0)
    loss_parts = join(reduced[img_share:slot])[:3]
    place = yl * Z + z
    own_image = x * share_cols + place * img_share
    own_text = x * text_share + place * txt_share

    def own(weight, gain, values, start):
        count = values.shape[0]
        used = lax.dynamic_slice_in_dim(weight, start, count, 0).astype(F32)
        return jnp.sum(values * used, axis=1) / lax.dynamic_slice_in_dim(gain, start, count, 0)

    small = jnp.concatenate(
        [
            own(img_weight, img_gain, reduced[:img_share], own_image),
            own(txt_weight, txt_gain, reduced[slot:], own_text),
            loss_parts,
        ]
    )
    small = small + swap(small, "co")
    small = small + swap(small, "yh")
    gains, loss_parts = small[: img_share + txt_share], small[img_share + txt_share :]
    ready = jnp.concatenate(
        [
            reduced[:img_share].astype(BF16),
            small_rows(gains, slot - img_share),
            reduced[slot:].astype(BF16),
        ],
        axis=0,
    )
    gathered = exchange(jnp.broadcast_to(ready, (16, *ready.shape)), ("yl", "z"))
    pieces = [gathered] + [lax.ppermute(gathered, "x", ring(k)) for k in range(1, 4)]
    image_grad, text_grad, gains = finish(
        jnp.stack(sources), pieces, img_weight.shape[0], txt_weight.shape[0]
    )
    return (
        loss_parts[0:1] / pair_count,
        image_grad,
        text_grad,
        gains[:, :, :img_share].reshape(-1),
        gains[:, :, img_share : img_share + txt_share].reshape(-1),
        loss_parts[1:2] * logit_scale,
        loss_parts[2:3],
    )


def solution(mesh):
    inner = Mesh(mesh.devices.reshape(2, Z, 4, 2, 2), ("yl", "z", "x", "yh", "co"))
    tensor = ("yh", "co")
    return jax.shard_map(
        local,
        mesh=inner,
        in_specs=(
            P(DP, None),
            P(DP, None),
            P(),
            P(),
            P(None, tensor),
            P(None, tensor),
            P(),
            P(),
            P(),
        ),
        out_specs=(P(), P(None, tensor), P(None, tensor), P(), P(), P(), P()),
        check_vma=False,
    )
```

```python
import jax
import jax.numpy as jnp
from jax import lax
from jax.experimental import pallas as pl
from jax.experimental.pallas import tpu as pltpu
from jax.sharding import Mesh, PartitionSpec as P

EPS = 1e-06
F32 = jnp.float32
BF16 = jnp.bfloat16
Z = 8
TEXT_Z = 4
DP = ("yl", "z", "x")
STEPS = 4


def hidden_rows(features, gain_vec):
    values = features.astype(F32)
    center = jnp.mean(values, axis=1, keepdims=True)
    spread = jnp.mean(values * values, axis=1, keepdims=True) - center * center
    scaled = (values - center) * lax.rsqrt(spread + EPS)
    return (scaled * gain_vec).astype(BF16)


def swap(value, axis):
    return lax.ppermute(value, axis, [(0, 1), (1, 0)])


def exchange(value, axes):
    return lax.all_to_all(value, axes, split_axis=0, concat_axis=0, tiled=True)


def split3(value):
    high = value.astype(BF16)
    rest = value - high.astype(F32)
    middle = rest.astype(BF16)
    return high, middle, (rest - middle.astype(F32)).astype(BF16)


def tile_kernel(
    factors, partner, columns, emb_i, emb_t, out_i, out_t, out_s, acc, sums
):
    step = pl.program_id(0)
    scale, shift = factors[0], factors[1]

    @pl.when(step == 0)
    def _():
        acc[...] = jnp.zeros_like(acc)
        sums[...] = jnp.zeros_like(sums)

    rows = jnp.concatenate(
        [
            jnp.concatenate([emb_i[0], emb_i[1]], axis=1),
            jnp.concatenate([emb_i[2], emb_i[3]], axis=1),
        ],
        axis=0,
    )
    texts = emb_t[...]
    high = emb_i.shape[1]
    half = emb_i.shape[2]
    place = lax.broadcasted_iota(jnp.int32, (2 * high, 1), 0)
    weight = jnp.where(place < high, factors[2], factors[3])
    similar = lax.dot_general(rows, texts, (((1,), (1,)), ((), ())), preferred_element_type=F32)
    logits = scale * similar + shift
    pair = partner[...] == columns[...]
    signed = jnp.where(pair, -logits, logits)
    small = jnp.exp(-jnp.abs(signed))
    total = 1.0 + small
    inverse = 1.0 / total
    sigmoid = jnp.where(signed >= 0, inverse, small * inverse)
    soft = jnp.maximum(signed, 0.0) + jnp.log(total) + (small - (total - 1.0)) * inverse
    grad = jnp.where(pair, -sigmoid, sigmoid) * weight
    sums[0:1] += jnp.sum(soft * weight, axis=0, keepdims=True)
    sums[1:2] += jnp.sum(grad * similar, axis=0, keepdims=True)
    sums[2:3] += jnp.sum(grad, axis=0, keepdims=True)
    rounded = grad.astype(BF16)
    acc[...] += lax.dot_general(rounded, rows, (((0,), (0,)), ((), ())), preferred_element_type=F32)
    grad_rows = jnp.dot(rounded, texts, preferred_element_type=F32)
    wide = rows.astype(F32)
    inner = jnp.sum(wide * grad_rows, axis=1, keepdims=True)
    result = (scale * (grad_rows - wide * inner)).astype(BF16)
    out_i[0] = result[:high, :half]
    out_i[1] = result[:high, half:]
    out_i[2] = result[high:, :half]
    out_i[3] = result[high:, half:]

    @pl.when(step == STEPS - 1)
    def _():
        texts = emb_t[...].astype(F32)
        grads = acc[...]
        inner = jnp.sum(texts * grads, axis=1, keepdims=True)
        out_t[...] = (scale * (grads - texts * inner)).astype(BF16)
        out_s[...] = jnp.broadcast_to(jnp.sum(sums[...], axis=1, keepdims=True), out_s.shape)


def tile_grads(factors, partner, columns, emb_i, emb_t):
    slabs, high, half = emb_i.shape
    block = slabs // STEPS
    count, width = emb_t.shape
    return pl.pallas_call(
        tile_kernel,
        grid=(STEPS,),
        in_specs=[
            pl.BlockSpec(memory_space=pltpu.SMEM),
            pl.BlockSpec((partner.shape[0] // STEPS, 1), lambda i: (i, 0)),
            pl.BlockSpec((1, count), lambda i: (0, 0)),
            pl.BlockSpec((block, high, half), lambda i: (i, 0, 0)),
            pl.BlockSpec((count, width), lambda i: (0, 0)),
        ],
        out_specs=[
            pl.BlockSpec((block, high, half), lambda i: (i, 0, 0)),
            pl.BlockSpec((count, width), lambda i: (0, 0)),
            pl.BlockSpec((8, 128), lambda i: (0, 0)),
        ],
        out_shape=[
            jax.ShapeDtypeStruct(emb_i.shape, BF16),
            jax.ShapeDtypeStruct(emb_t.shape, BF16),
            jax.ShapeDtypeStruct((8, 128), F32),
        ],
        scratch_shapes=[pltpu.VMEM((count, width), F32), pltpu.VMEM((8, count), F32)],
        compiler_params=pltpu.CompilerParams(vmem_limit_bytes=40 * 1024 * 1024),
    )(factors, partner, columns, emb_i, emb_t)


def half_place(half, j):
    return TEXT_Z + j if half else TEXT_Z - 1 - j


def turn(k):
    return [
        (half_place(half, j), half_place(half, (j + k) % TEXT_Z))
        for half in range(2)
        for j in range(TEXT_Z)
    ]


def finish_kernel(places, first, second, third, fourth, out_i, out_t, rows):
    image_rows = rows.shape[0] // 16
    text_rows = out_t.shape[0] // 64
    padded = first.shape[1] - text_rows
    for k, piece in enumerate((first, second, third, fourth)):
        place = places[k]
        for s in range(16):
            values = piece[s].astype(F32)
            rows[s * image_rows : (s + 1) * image_rows] = values[:image_rows]
            start = pl.multiple_of(place * (16 * text_rows) + s * text_rows, 8)
            out_t[pl.ds(start, text_rows)] = values[padded:]
        start = pl.multiple_of(place * (16 * image_rows), 8)
        out_i[pl.ds(start, 16 * image_rows)] = rows[...]


def finish(places, pieces, image_total, text_total):
    cols = pieces[0].shape[2]
    whole = pl.BlockSpec(memory_space=pltpu.VMEM)
    return pl.pallas_call(
        finish_kernel,
        in_specs=[pl.BlockSpec(memory_space=pltpu.SMEM)] + [whole] * 4,
        out_specs=[whole] * 2,
        out_shape=[
            jax.ShapeDtypeStruct((image_total, cols), F32),
            jax.ShapeDtypeStruct((text_total, cols), F32),
        ],
        scratch_shapes=[pltpu.VMEM((image_total // 4, cols), F32)],
        compiler_params=pltpu.CompilerParams(vmem_limit_bytes=24 * 1024 * 1024),
    )(places, *pieces)


def ring(k):
    return [(i, (i + k) % 4) for i in range(4)]


def y_move(value, k):
    return lax.ppermute(value, ("yl", "yh"), [(i, i ^ k) for i in range(4)])


def pick(value, index, axis=0):
    return lax.dynamic_index_in_dim(value, index, axis, keepdims=False)


def local(
    img_feats, txt_feats, img_gain, txt_gain, img_weight, txt_weight, log_scale, bias, pair_perm
):
    yl, z, x = lax.axis_index("yl"), lax.axis_index("z"), lax.axis_index("x")
    yh, core = lax.axis_index("yh"), lax.axis_index("co")
    pair_count = pair_perm.shape[0]
    img_count, txt_count = img_feats.shape[0], txt_feats.shape[0]
    img_half, txt_half = img_count // 2, txt_count // 2
    piece = txt_half // 4
    is_text = (yl == 1) & (z >= TEXT_Z)
    near = jnp.where(z >= TEXT_Z, z - TEXT_Z, TEXT_Z - 1 - z)
    sources = [jnp.mod(x - k + 4, 4) for k in range(4)]
    targets = [jnp.mod(x + k, 4) for k in range(4)]

    text_hidden = hidden_rows(txt_feats, txt_gain)
    image_hidden = hidden_rows(img_feats, img_gain)
    share_cols = image_hidden.shape[1] // 4
    parts = jnp.stack(
        [image_hidden[:, i * share_cols : (i + 1) * share_cols] for i in range(4)]
    )
    hidden_x = [pick(parts, x)]
    hidden_x += [lax.ppermute(pick(parts, targets[k]), "x", ring(k)) for k in range(1, 4)]

    text_proj = jnp.dot(text_hidden, txt_weight, preferred_element_type=F32)
    image_proj = jnp.dot(image_hidden, img_weight, preferred_element_type=F32)
    squares = jnp.concatenate(
        [jnp.sum(text_proj * text_proj, axis=1), jnp.sum(image_proj * image_proj, axis=1)]
    )
    squares = squares + swap(squares, "co")
    squares = squares + swap(squares, "yh")
    squares, hidden_x[1] = lax.optimization_barrier((squares, hidden_x[1]))
    norms = jnp.sqrt(squares + EPS)[:, None]
    text_norm, image_norm = norms[:txt_count], norms[txt_count:]
    text_emb = (text_proj / text_norm).astype(BF16)
    image_emb = (image_proj / image_norm).astype(BF16)

    def halves(index):
        return jnp.concatenate(
            [
                lax.dynamic_slice_in_dim(image_emb, index * img_half, img_half, 0),
                lax.dynamic_slice_in_dim(text_emb, index * txt_half, txt_half, 0),
            ],
            axis=0,
        )

    kept = halves(core)
    taken = swap(halves(1 - core), "co")
    both = jnp.where(
        core == 0,
        jnp.concatenate([kept, taken], axis=1),
        jnp.concatenate([taken, kept], axis=1),
    )
    width = both.shape[1]
    image_own = both[:img_half]
    text_own = both[img_half:].reshape(4, piece, width)

    got = []
    for k in range(1, 4):
        target = jnp.bitwise_xor(yl * 2 + yh, k)
        got.append(y_move(jnp.concatenate([image_own, pick(text_own, target)], axis=0), k))
    got, hidden_x = lax.optimization_barrier((got, hidden_x))
    slabs = jnp.stack([image_own] + [g[:img_half] for g in got])
    mine = jnp.where(yl == 1, pick(text_own, yl * 2 + yh), got[1][img_half:])
    other = jnp.where(yl == 1, got[0][img_half:], got[2][img_half:])
    chunk = jnp.concatenate([mine, other], axis=1)
    mirror = [(a, Z - 1 - a) for a in range(TEXT_Z, Z)]
    chunk = jnp.where(z >= TEXT_Z, chunk, lax.ppermute(chunk, "z", mirror))
    image_all = jnp.concatenate([slabs] + [lax.ppermute(slabs, "x", ring(k)) for k in range(1, 4)])
    chunks = jnp.stack([chunk] + [lax.ppermute(chunk, "z", turn(k)) for k in range(1, TEXT_Z)])
    text_tile = jnp.stack([chunks, swap(chunks, "co")])
    text_tile = text_tile.reshape(2 * TEXT_Z * piece, 2 * width)

    quarter = yl * 2 + yh
    order = jnp.arange(TEXT_Z, dtype=jnp.int32)
    group = jnp.mod(near - order + TEXT_Z, TEXT_Z) * 4 + x
    columns = (
        group[None, :, None] * txt_count
        + jnp.mod(core + jnp.arange(2, dtype=jnp.int32), 2)[:, None, None] * txt_half
        + quarter * piece
        + jnp.arange(piece, dtype=jnp.int32)[None, None, :]
    ).reshape(1, -1)
    padded = jnp.concatenate([pair_perm, jnp.full((16 * img_count,), -1, jnp.int32)])
    padded = pick(pick(padded.reshape(2, Z, 4, 2, img_half), z, 1), core, 2)
    padded = jnp.where(yl == 0, padded, padded[::-1])
    partner = jnp.stack([pick(padded, source, 1) for source in sources]).reshape(-1, 1)
    logit_scale = jnp.exp(log_scale[0])
    weights = [
        jnp.where((side == 1) & (z >= TEXT_Z), 0.0, 1.0).astype(F32) for side in (yl, 1 - yl)
    ]
    factors = jnp.stack([logit_scale, bias[0], *weights])

    image_part, text_part, part_sums = tile_grads(factors, partner, columns, image_all, text_tile)

    text_part = text_part.reshape(2, TEXT_Z, piece, 2 * width)
    both = text_part[0].astype(F32) + swap(text_part[1], "co").astype(F32)
    rounded = both.astype(BF16)
    image_part = image_part.reshape(4, 4, img_half, width)
    text_got = [lax.ppermute(rounded[k], "z", turn(TEXT_Z - k)) for k in range(1, TEXT_Z)]
    image_near = [lax.ppermute(image_part[k], "x", ring(-k)) for k in (1, 3)]
    text_got[0], image_far = lax.optimization_barrier((text_got[0], image_part[2]))
    image_far = lax.ppermute(image_far, "x", ring(-2))
    text_got, image_near, image_far = lax.optimization_barrier((text_got, image_near, image_far))
    text_sum = both[0]
    for g in text_got:
        text_sum = text_sum + g.astype(F32)
    text_round = text_sum.astype(BF16)
    text_mirror = lax.ppermute(text_round, "z", [(b, a) for a, b in mirror])
    image_sum = image_part[0].astype(F32)
    for g in (*image_near, image_far):
        image_sum = image_sum + g.astype(F32)

    image_round = image_sum.astype(BF16)
    image_sum = image_sum[0]
    for k in range(1, 4):
        image_sum = image_sum + y_move(image_round[k], k).astype(F32)
    text_sum, text_mirror, image_sum = lax.optimization_barrier(
        (text_sum, text_mirror, image_sum)
    )
    text_sum = (text_sum + text_mirror.astype(F32)).astype(BF16)
    same, cross = text_sum[:, :width], text_sum[:, width:]
    across, straight, diagonal = [y_move(cross if k & 1 else same, k) for k in range(1, 4)]
    cols = width // 2

    def join_cores(rows):
        kept = lax.dynamic_slice_in_dim(rows, core * cols, cols, 1)
        taken = swap(lax.dynamic_slice_in_dim(rows, (1 - core) * cols, cols, 1), "co")
        return jnp.where(
            core == 0,
            jnp.concatenate([kept, taken], axis=0),
            jnp.concatenate([taken, kept], axis=0),
        )

    image_rows = image_sum / lax.dynamic_slice_in_dim(image_norm, core * img_half, img_half, 0)
    image_du = join_cores(image_rows.astype(BF16))
    du_x = [image_du] + [lax.ppermute(image_du, "x", ring(k)) for k in (1, 3)]
    across, straight, diagonal, du_x = lax.optimization_barrier(
        (across, straight, diagonal, du_x)
    )
    du_x.insert(2, lax.ppermute(image_du, "x", ring(2)))
    transposed = (((0,), (0,)), ((), ()))

    text_rows = jnp.where(
        yh == 0,
        jnp.concatenate([straight, diagonal, same, across], axis=0),
        jnp.concatenate([diagonal, straight, across, same], axis=0),
    )
    text_rows = text_rows.astype(F32) / lax.dynamic_slice_in_dim(
        text_norm, core * txt_half, txt_half, 0
    )
    text_du = join_cores(jnp.where(is_text, text_rows, 0.0).astype(BF16))
    text_weight = lax.dot_general(text_hidden, text_du, transposed, preferred_element_type=F32)
    text_share = text_weight.shape[0] // 4
    text_weight = text_weight.reshape(4, text_share, cols)
    text_weight, du_x = lax.optimization_barrier((text_weight, du_x))
    loss_parts = part_sums[:3, 0]

    def small_rows(values, count):
        rows = jnp.stack(split3(values), axis=0)
        return jnp.pad(rows, ((0, count - 3), (0, cols - values.shape[0])))

    def join(rows):
        return rows[0] + rows[1] + rows[2]

    tail = small_rows(loss_parts, 16)
    got = [
        lax.ppermute(
            jnp.concatenate([pick(text_weight, targets[k]).astype(BF16), tail], axis=0),
            "x",
            ring(k),
        )
        for k in range(1, 4)
    ]
    image_weight = lax.dot_general(
        jnp.concatenate(hidden_x), jnp.concatenate(du_x), transposed, preferred_element_type=F32
    )
    text_weight = pick(text_weight, x)
    for g in got:
        text_weight = text_weight + g[:text_share].astype(F32)
        loss_parts = loss_parts + join(g[text_share:].astype(F32))[:3]

    img_share, txt_share = share_cols // 16, text_share // 16
    slot = 32
    block = jnp.concatenate(
        [
            image_weight.astype(BF16).reshape(16, img_share, cols),
            jnp.broadcast_to(
                small_rows(loss_parts, slot - img_share), (16, slot - img_share, cols)
            ),
            text_weight.astype(BF16).reshape(16, txt_share, cols),
        ],
        axis=1,
    )
    reduced = jnp.sum(exchange(block, ("yl", "z")).astype(F32), axis=0)
    loss_parts = join(reduced[img_share:slot])[:3]
    place = yl * Z + z
    own_image = x * share_cols + place * img_share
    own_text = x * text_share + place * txt_share

    def own(weight, gain, values, start):
        count = values.shape[0]
        used = lax.dynamic_slice_in_dim(weight, start, count, 0).astype(F32)
        return jnp.sum(values * used, axis=1) / lax.dynamic_slice_in_dim(gain, start, count, 0)

    gains = jnp.concatenate(
        [
            own(img_weight, img_gain, reduced[:img_share], own_image),
            own(txt_weight, txt_gain, reduced[slot:], own_text),
        ]
    )
    ready = jnp.concatenate(
        [
            reduced[:img_share].astype(BF16),
            small_rows(gains, slot - img_share),
            reduced[slot:].astype(BF16),
        ],
        axis=0,
    )
    gathered = exchange(jnp.broadcast_to(ready, (16, *ready.shape)), ("yl", "z"))
    pieces = [lax.ppermute(gathered, "x", ring(k)) for k in (1, 3)]

    count = img_share + txt_share
    small = jnp.sum(gathered[:, img_share : img_share + 3, :count].astype(F32), axis=1)
    small = jnp.concatenate([small.reshape(-1), loss_parts])
    small = small + swap(small, "co")
    small = small + swap(small, "yh")
    small, pieces, far = lax.optimization_barrier((small, pieces, gathered))
    far = lax.ppermute(far, "x", ring(2))
    gains, loss_parts = small[: 16 * count], small[16 * count :]
    gains = jnp.stack([gains] + [lax.ppermute(gains, "x", ring(k)) for k in range(1, 4)])
    gains = jnp.stack([pick(gains, jnp.mod(x - a + 4, 4)) for a in range(4)])
    gains = gains.reshape(64, count)
    image_grad, text_grad = finish(
        jnp.stack(sources),
        [gathered, pieces[0], far, pieces[1]],
        img_weight.shape[0],
        txt_weight.shape[0],
    )
    return (
        loss_parts[0:1] / pair_count,
        image_grad,
        text_grad,
        gains[:, :img_share].reshape(-1),
        gains[:, img_share:].reshape(-1),
        loss_parts[1:2] * logit_scale,
        loss_parts[2:3],
    )


def solution(mesh):
    inner = Mesh(mesh.devices.reshape(2, Z, 4, 2, 2), ("yl", "z", "x", "yh", "co"))
    tensor = ("yh", "co")
    return jax.shard_map(
        local,
        mesh=inner,
        in_specs=(
            P(DP, None),
            P(DP, None),
            P(),
            P(),
            P(None, tensor),
            P(None, tensor),
            P(),
            P(),
            P(),
        ),
        out_specs=(P(), P(None, tensor), P(None, tensor), P(), P(), P(), P()),
        check_vma=False,
    )
```

```python
import jax
import jax.numpy as jnp
from jax import lax
from jax.experimental import pallas as pl
from jax.experimental.pallas import tpu as pltpu
from jax.sharding import Mesh, PartitionSpec as P

EPS = 1e-06
F32 = jnp.float32
BF16 = jnp.bfloat16
Z = 8
TEXT_Z = 4
DP = ("yl", "z", "x")
STEPS = 4


def hidden_rows(features, gain_vec):
    values = features.astype(F32)
    center = jnp.mean(values, axis=1, keepdims=True)
    spread = jnp.mean(values * values, axis=1, keepdims=True) - center * center
    scaled = (values - center) * lax.rsqrt(spread + EPS)
    return (scaled * gain_vec).astype(BF16)


def swap(value, axis):
    return lax.ppermute(value, axis, [(0, 1), (1, 0)])


def exchange(value, axes):
    return lax.all_to_all(value, axes, split_axis=0, concat_axis=0, tiled=True)


def split3(value):
    high = value.astype(BF16)
    rest = value - high.astype(F32)
    middle = rest.astype(BF16)
    return high, middle, (rest - middle.astype(F32)).astype(BF16)


def tile_kernel(
    factors, partner, columns, emb_i, emb_t, out_i, out_t, out_s, acc, sums
):
    step = pl.program_id(0)
    scale, shift = factors[0], factors[1]

    @pl.when(step == 0)
    def _():
        acc[...] = jnp.zeros_like(acc)
        sums[...] = jnp.zeros_like(sums)

    rows = jnp.concatenate(
        [
            jnp.concatenate([emb_i[0], emb_i[1]], axis=1),
            jnp.concatenate([emb_i[2], emb_i[3]], axis=1),
        ],
        axis=0,
    )
    texts = emb_t[...]
    high = emb_i.shape[1]
    half = emb_i.shape[2]
    place = lax.broadcasted_iota(jnp.int32, (2 * high, 1), 0)
    weight = jnp.where(place < high, factors[2], factors[3])
    similar = lax.dot_general(rows, texts, (((1,), (1,)), ((), ())), preferred_element_type=F32)
    logits = scale * similar + shift
    pair = partner[...] == columns[...]
    signed = jnp.where(pair, -logits, logits)
    small = jnp.exp(-jnp.abs(signed))
    total = 1.0 + small
    inverse = 1.0 / total
    sigmoid = jnp.where(signed >= 0, inverse, small * inverse)
    soft = jnp.maximum(signed, 0.0) + jnp.log(total) + (small - (total - 1.0)) * inverse
    grad = jnp.where(pair, -sigmoid, sigmoid) * weight
    sums[0:1] += jnp.sum(soft * weight, axis=0, keepdims=True)
    sums[1:2] += jnp.sum(grad * similar, axis=0, keepdims=True)
    sums[2:3] += jnp.sum(grad, axis=0, keepdims=True)
    rounded = grad.astype(BF16)
    acc[...] += lax.dot_general(rounded, rows, (((0,), (0,)), ((), ())), preferred_element_type=F32)
    grad_rows = jnp.dot(rounded, texts, preferred_element_type=F32)
    wide = rows.astype(F32)
    inner = jnp.sum(wide * grad_rows, axis=1, keepdims=True)
    result = (scale * (grad_rows - wide * inner)).astype(BF16)
    out_i[0] = result[:high, :half]
    out_i[1] = result[:high, half:]
    out_i[2] = result[high:, :half]
    out_i[3] = result[high:, half:]

    @pl.when(step == STEPS - 1)
    def _():
        texts = emb_t[...].astype(F32)
        grads = acc[...]
        inner = jnp.sum(texts * grads, axis=1, keepdims=True)
        out_t[...] = (scale * (grads - texts * inner)).astype(BF16)
        out_s[...] = jnp.broadcast_to(jnp.sum(sums[...], axis=1, keepdims=True), out_s.shape)


def tile_grads(factors, partner, columns, emb_i, emb_t):
    slabs, high, half = emb_i.shape
    block = slabs // STEPS
    count, width = emb_t.shape
    return pl.pallas_call(
        tile_kernel,
        grid=(STEPS,),
        in_specs=[
            pl.BlockSpec(memory_space=pltpu.SMEM),
            pl.BlockSpec((partner.shape[0] // STEPS, 1), lambda i: (i, 0)),
            pl.BlockSpec((1, count), lambda i: (0, 0)),
            pl.BlockSpec((block, high, half), lambda i: (i, 0, 0)),
            pl.BlockSpec((count, width), lambda i: (0, 0)),
        ],
        out_specs=[
            pl.BlockSpec((block, high, half), lambda i: (i, 0, 0)),
            pl.BlockSpec((count, width), lambda i: (0, 0)),
            pl.BlockSpec((8, 128), lambda i: (0, 0)),
        ],
        out_shape=[
            jax.ShapeDtypeStruct(emb_i.shape, BF16),
            jax.ShapeDtypeStruct(emb_t.shape, BF16),
            jax.ShapeDtypeStruct((8, 128), F32),
        ],
        scratch_shapes=[pltpu.VMEM((count, width), F32), pltpu.VMEM((8, count), F32)],
        compiler_params=pltpu.CompilerParams(vmem_limit_bytes=40 * 1024 * 1024),
    )(factors, partner, columns, emb_i, emb_t)


def half_place(half, j):
    return TEXT_Z + j if half else TEXT_Z - 1 - j


def turn(k):
    return [
        (half_place(half, j), half_place(half, (j + k) % TEXT_Z))
        for half in range(2)
        for j in range(TEXT_Z)
    ]


def finish_kernel(places, first, second, third, fourth, out_i, out_t, rows):
    image_rows = rows.shape[0] // 16
    text_rows = out_t.shape[0] // 64
    padded = first.shape[1] - text_rows
    for k, piece in enumerate((first, second, third, fourth)):
        place = places[k]
        for s in range(16):
            values = piece[s].astype(F32)
            rows[s * image_rows : (s + 1) * image_rows] = values[:image_rows]
            start = pl.multiple_of(place * (16 * text_rows) + s * text_rows, 8)
            out_t[pl.ds(start, text_rows)] = values[padded:]
        start = pl.multiple_of(place * (16 * image_rows), 8)
        out_i[pl.ds(start, 16 * image_rows)] = rows[...]


def finish(places, pieces, image_total, text_total):
    cols = pieces[0].shape[2]
    whole = pl.BlockSpec(memory_space=pltpu.VMEM)
    return pl.pallas_call(
        finish_kernel,
        in_specs=[pl.BlockSpec(memory_space=pltpu.SMEM)] + [whole] * 4,
        out_specs=[whole] * 2,
        out_shape=[
            jax.ShapeDtypeStruct((image_total, cols), F32),
            jax.ShapeDtypeStruct((text_total, cols), F32),
        ],
        scratch_shapes=[pltpu.VMEM((image_total // 4, cols), F32)],
        compiler_params=pltpu.CompilerParams(vmem_limit_bytes=24 * 1024 * 1024),
    )(places, *pieces)


def ring(k):
    return [(i, (i + k) % 4) for i in range(4)]


def y_move(value, k):
    return lax.ppermute(value, ("yl", "yh"), [(i, i ^ k) for i in range(4)])


def pick(value, index, axis=0):
    return lax.dynamic_index_in_dim(value, index, axis, keepdims=False)


def local(
    img_feats, txt_feats, img_gain, txt_gain, img_weight, txt_weight, log_scale, bias, pair_perm
):
    yl, z, x = lax.axis_index("yl"), lax.axis_index("z"), lax.axis_index("x")
    yh, core = lax.axis_index("yh"), lax.axis_index("co")
    pair_count = pair_perm.shape[0]
    img_count, txt_count = img_feats.shape[0], txt_feats.shape[0]
    img_half, txt_half = img_count // 2, txt_count // 2
    piece = txt_half // 4
    is_text = (yl == 1) & (z >= TEXT_Z)
    near = jnp.where(z >= TEXT_Z, z - TEXT_Z, TEXT_Z - 1 - z)
    sources = [jnp.mod(x - k + 4, 4) for k in range(4)]
    targets = [jnp.mod(x + k, 4) for k in range(4)]

    text_hidden = hidden_rows(txt_feats, txt_gain)
    image_hidden = hidden_rows(img_feats, img_gain)
    share_cols = image_hidden.shape[1] // 4
    parts = jnp.stack(
        [image_hidden[:, i * share_cols : (i + 1) * share_cols] for i in range(4)]
    )
    text_proj = jnp.dot(text_hidden, txt_weight, preferred_element_type=F32)
    image_proj = jnp.dot(image_hidden, img_weight, preferred_element_type=F32)
    squares = jnp.concatenate(
        [jnp.sum(text_proj * text_proj, axis=1), jnp.sum(image_proj * image_proj, axis=1)]
    )
    squares = squares + swap(squares, "co")
    squares = squares + swap(squares, "yh")
    norms = jnp.sqrt(squares + EPS)[:, None]
    text_norm, image_norm = norms[:txt_count], norms[txt_count:]
    text_emb = (text_proj / text_norm).astype(BF16)
    image_emb = (image_proj / image_norm).astype(BF16)

    def halves(index):
        return jnp.concatenate(
            [
                lax.dynamic_slice_in_dim(image_emb, index * img_half, img_half, 0),
                lax.dynamic_slice_in_dim(text_emb, index * txt_half, txt_half, 0),
            ],
            axis=0,
        )

    kept = halves(core)
    taken = swap(halves(1 - core), "co")
    both = jnp.where(
        core == 0,
        jnp.concatenate([kept, taken], axis=1),
        jnp.concatenate([taken, kept], axis=1),
    )
    parts, both = lax.optimization_barrier((parts, both))
    hidden_x = [pick(parts, x)]
    hidden_x += [lax.ppermute(pick(parts, targets[k]), "x", ring(k)) for k in range(1, 4)]
    width = both.shape[1]
    image_own = both[:img_half]
    text_own = both[img_half:].reshape(4, piece, width)

    got = []
    for k in range(1, 4):
        target = jnp.bitwise_xor(yl * 2 + yh, k)
        got.append(y_move(jnp.concatenate([image_own, pick(text_own, target)], axis=0), k))
    got, hidden_x[1], hidden_x[3] = lax.optimization_barrier((got, hidden_x[1], hidden_x[3]))
    slabs = jnp.stack([image_own] + [g[:img_half] for g in got])
    mine = jnp.where(yl == 1, pick(text_own, yl * 2 + yh), got[1][img_half:])
    other = jnp.where(yl == 1, got[0][img_half:], got[2][img_half:])
    chunk = jnp.concatenate([mine, other], axis=1)
    mirror = [(a, Z - 1 - a) for a in range(TEXT_Z, Z)]
    chunk = jnp.where(z >= TEXT_Z, chunk, lax.ppermute(chunk, "z", mirror))
    image_all = jnp.concatenate([slabs] + [lax.ppermute(slabs, "x", ring(k)) for k in range(1, 4)])
    chunks = jnp.stack([chunk] + [lax.ppermute(chunk, "z", turn(k)) for k in range(1, TEXT_Z)])
    chunks, hidden_x[2] = lax.optimization_barrier((chunks, hidden_x[2]))
    text_tile = jnp.stack([chunks, swap(chunks, "co")])
    text_tile = text_tile.reshape(2 * TEXT_Z * piece, 2 * width)

    quarter = yl * 2 + yh
    order = jnp.arange(TEXT_Z, dtype=jnp.int32)
    group = jnp.mod(near - order + TEXT_Z, TEXT_Z) * 4 + x
    columns = (
        group[None, :, None] * txt_count
        + jnp.mod(core + jnp.arange(2, dtype=jnp.int32), 2)[:, None, None] * txt_half
        + quarter * piece
        + jnp.arange(piece, dtype=jnp.int32)[None, None, :]
    ).reshape(1, -1)
    padded = jnp.concatenate([pair_perm, jnp.full((16 * img_count,), -1, jnp.int32)])
    padded = pick(pick(padded.reshape(2, Z, 4, 2, img_half), z, 1), core, 2)
    padded = jnp.where(yl == 0, padded, padded[::-1])
    partner = jnp.stack([pick(padded, source, 1) for source in sources]).reshape(-1, 1)
    logit_scale = jnp.exp(log_scale[0])
    weights = [
        jnp.where((side == 1) & (z >= TEXT_Z), 0.0, 1.0).astype(F32) for side in (yl, 1 - yl)
    ]
    factors = jnp.stack([logit_scale, bias[0], *weights])

    image_part, text_part, part_sums = tile_grads(factors, partner, columns, image_all, text_tile)

    text_part = text_part.reshape(2, TEXT_Z, piece, 2 * width)
    both = text_part[0].astype(F32) + swap(text_part[1], "co").astype(F32)
    rounded = both.astype(BF16)
    image_part = image_part.reshape(4, 4, img_half, width)
    text_got = [lax.ppermute(rounded[k], "z", turn(TEXT_Z - k)) for k in range(1, TEXT_Z)]
    image_near = [lax.ppermute(image_part[k], "x", ring(-k)) for k in (1, 3)]
    text_got[0], image_far = lax.optimization_barrier((text_got[0], image_part[2]))
    image_far = lax.ppermute(image_far, "x", ring(-2))
    text_got, image_near, image_far = lax.optimization_barrier((text_got, image_near, image_far))
    text_sum = both[0]
    for g in text_got:
        text_sum = text_sum + g.astype(F32)
    text_round = text_sum.astype(BF16)
    text_mirror = lax.ppermute(text_round, "z", [(b, a) for a, b in mirror])
    image_sum = image_part[0].astype(F32)
    for g in (*image_near, image_far):
        image_sum = image_sum + g.astype(F32)

    image_round = image_sum.astype(BF16)
    image_sum = image_sum[0]
    for k in range(1, 4):
        image_sum = image_sum + y_move(image_round[k], k).astype(F32)
    text_sum, text_mirror, image_sum = lax.optimization_barrier(
        (text_sum, text_mirror, image_sum)
    )
    text_sum = (text_sum + text_mirror.astype(F32)).astype(BF16)
    same, cross = text_sum[:, :width], text_sum[:, width:]
    across, straight, diagonal = [y_move(cross if k & 1 else same, k) for k in range(1, 4)]
    cols = width // 2

    def join_cores(rows):
        kept = lax.dynamic_slice_in_dim(rows, core * cols, cols, 1)
        taken = swap(lax.dynamic_slice_in_dim(rows, (1 - core) * cols, cols, 1), "co")
        return jnp.where(
            core == 0,
            jnp.concatenate([kept, taken], axis=0),
            jnp.concatenate([taken, kept], axis=0),
        )

    image_rows = image_sum / lax.dynamic_slice_in_dim(image_norm, core * img_half, img_half, 0)
    image_du = join_cores(image_rows.astype(BF16))
    du_x = [image_du] + [lax.ppermute(image_du, "x", ring(k)) for k in (1, 3)]
    across, straight, diagonal, du_x = lax.optimization_barrier(
        (across, straight, diagonal, du_x)
    )
    du_x.insert(2, lax.ppermute(image_du, "x", ring(2)))
    transposed = (((0,), (0,)), ((), ()))

    text_rows = jnp.where(
        yh == 0,
        jnp.concatenate([straight, diagonal, same, across], axis=0),
        jnp.concatenate([diagonal, straight, across, same], axis=0),
    )
    text_rows = text_rows.astype(F32) / lax.dynamic_slice_in_dim(
        text_norm, core * txt_half, txt_half, 0
    )
    text_du = join_cores(jnp.where(is_text, text_rows, 0.0).astype(BF16))
    text_weight = lax.dot_general(text_hidden, text_du, transposed, preferred_element_type=F32)
    text_share = text_weight.shape[0] // 4
    text_weight = text_weight.reshape(4, text_share, cols)
    loss_parts = part_sums[:3, 0]

    def small_rows(values, count):
        rows = jnp.stack(split3(values), axis=0)
        return jnp.pad(rows, ((0, count - 3), (0, cols - values.shape[0])))

    def join(rows):
        return rows[0] + rows[1] + rows[2]

    tail = small_rows(loss_parts, 16)
    got = [
        lax.ppermute(
            jnp.concatenate([pick(text_weight, targets[k]).astype(BF16), tail], axis=0),
            "x",
            ring(k),
        )
        for k in range(1, 4)
    ]
    image_weight = lax.dot_general(
        jnp.concatenate(hidden_x), jnp.concatenate(du_x), transposed, preferred_element_type=F32
    )
    text_weight = pick(text_weight, x)
    for g in got:
        text_weight = text_weight + g[:text_share].astype(F32)
        loss_parts = loss_parts + join(g[text_share:].astype(F32))[:3]

    img_share, txt_share = share_cols // 16, text_share // 16
    slot = 32
    block = jnp.concatenate(
        [
            image_weight.astype(BF16).reshape(16, img_share, cols),
            jnp.broadcast_to(
                small_rows(loss_parts, slot - img_share), (16, slot - img_share, cols)
            ),
            text_weight.astype(BF16).reshape(16, txt_share, cols),
        ],
        axis=1,
    )
    reduced = jnp.sum(exchange(block, ("yl", "z")).astype(F32), axis=0)
    loss_parts = join(reduced[img_share:slot])[:3]
    place = yl * Z + z
    own_image = x * share_cols + place * img_share
    own_text = x * text_share + place * txt_share

    def own(weight, gain, values, start):
        count = values.shape[0]
        used = lax.dynamic_slice_in_dim(weight, start, count, 0).astype(F32)
        return jnp.sum(values * used, axis=1) / lax.dynamic_slice_in_dim(gain, start, count, 0)

    gains = jnp.concatenate(
        [
            own(img_weight, img_gain, reduced[:img_share], own_image),
            own(txt_weight, txt_gain, reduced[slot:], own_text),
        ]
    )
    ready = jnp.concatenate(
        [
            reduced[:img_share].astype(BF16),
            small_rows(gains, slot - img_share),
            reduced[slot:].astype(BF16),
        ],
        axis=0,
    )
    gathered = exchange(jnp.broadcast_to(ready, (16, *ready.shape)), ("yl", "z"))
    pieces = [lax.ppermute(gathered, "x", ring(k)) for k in range(1, 4)]

    count = img_share + txt_share
    small = jnp.sum(gathered[:, img_share : img_share + 3, :count].astype(F32), axis=1)
    small = jnp.concatenate([small.reshape(-1), loss_parts])
    small = small + swap(small, "co")
    small = small + swap(small, "yh")
    small, pieces[0], pieces[2] = lax.optimization_barrier((small, pieces[0], pieces[2]))
    gains, loss_parts = small[: 16 * count], small[16 * count :]
    gains = jnp.stack([gains] + [lax.ppermute(gains, "x", ring(k)) for k in range(1, 4)])
    gains = jnp.stack([pick(gains, jnp.mod(x - a + 4, 4)) for a in range(4)])
    gains = gains.reshape(64, count)
    image_grad, text_grad = finish(
        jnp.stack(sources),
        [gathered, *pieces],
        img_weight.shape[0],
        txt_weight.shape[0],
    )
    return (
        loss_parts[0:1] / pair_count,
        image_grad,
        text_grad,
        gains[:, :img_share].reshape(-1),
        gains[:, img_share:].reshape(-1),
        loss_parts[1:2] * logit_scale,
        loss_parts[2:3],
    )


def solution(mesh):
    inner = Mesh(mesh.devices.reshape(2, Z, 4, 2, 2), ("yl", "z", "x", "yh", "co"))
    tensor = ("yh", "co")
    return jax.shard_map(
        local,
        mesh=inner,
        in_specs=(
            P(DP, None),
            P(DP, None),
            P(),
            P(),
            P(None, tensor),
            P(None, tensor),
            P(),
            P(),
            P(),
        ),
        out_specs=(P(), P(None, tensor), P(None, tensor), P(), P(), P(), P()),
        check_vma=False,
    )
```

```python
import jax
import jax.numpy as jnp
from jax import lax
from jax.experimental import pallas as pl
from jax.experimental.pallas import tpu as pltpu
from jax.sharding import Mesh, PartitionSpec as P

EPS = 1e-06
F32 = jnp.float32
BF16 = jnp.bfloat16
Z = 8
TEXT_Z = 4
DP = ("yl", "z", "x")
STEPS = 4


def hidden_rows(features, gain_vec):
    values = features.astype(F32)
    center = jnp.mean(values, axis=1, keepdims=True)
    spread = jnp.mean(values * values, axis=1, keepdims=True) - center * center
    scaled = (values - center) * lax.rsqrt(spread + EPS)
    return (scaled * gain_vec).astype(BF16)


def swap(value, axis):
    return lax.ppermute(value, axis, [(0, 1), (1, 0)])


def exchange(value, axes):
    return lax.all_to_all(value, axes, split_axis=0, concat_axis=0, tiled=True)


def split3(value):
    high = value.astype(BF16)
    rest = value - high.astype(F32)
    middle = rest.astype(BF16)
    return high, middle, (rest - middle.astype(F32)).astype(BF16)


def tile_kernel(
    factors, partner, columns, emb_i, emb_t, out_i, out_t, out_s, acc, sums
):
    step = pl.program_id(0)
    scale, shift = factors[0], factors[1]

    @pl.when(step == 0)
    def _():
        acc[...] = jnp.zeros_like(acc)
        sums[...] = jnp.zeros_like(sums)

    rows = jnp.concatenate(
        [
            jnp.concatenate([emb_i[0], emb_i[1]], axis=1),
            jnp.concatenate([emb_i[2], emb_i[3]], axis=1),
        ],
        axis=0,
    )
    texts = emb_t[...]
    high = emb_i.shape[1]
    half = emb_i.shape[2]
    place = lax.broadcasted_iota(jnp.int32, (2 * high, 1), 0)
    weight = jnp.where(place < high, factors[2], factors[3])
    similar = lax.dot_general(rows, texts, (((1,), (1,)), ((), ())), preferred_element_type=F32)
    logits = scale * similar + shift
    pair = partner[...] == columns[...]
    signed = jnp.where(pair, -logits, logits)
    small = jnp.exp(-jnp.abs(signed))
    total = 1.0 + small
    inverse = 1.0 / total
    sigmoid = jnp.where(signed >= 0, inverse, small * inverse)
    soft = jnp.maximum(signed, 0.0) + jnp.log(total) + (small - (total - 1.0)) * inverse
    grad = jnp.where(pair, -sigmoid, sigmoid) * weight
    sums[0:1] += jnp.sum(soft * weight, axis=0, keepdims=True)
    sums[1:2] += jnp.sum(grad * similar, axis=0, keepdims=True)
    sums[2:3] += jnp.sum(grad, axis=0, keepdims=True)
    rounded = grad.astype(BF16)
    acc[...] += lax.dot_general(rounded, rows, (((0,), (0,)), ((), ())), preferred_element_type=F32)
    grad_rows = jnp.dot(rounded, texts, preferred_element_type=F32)
    wide = rows.astype(F32)
    inner = jnp.sum(wide * grad_rows, axis=1, keepdims=True)
    result = (scale * (grad_rows - wide * inner)).astype(BF16)
    out_i[0] = result[:high, :half]
    out_i[1] = result[:high, half:]
    out_i[2] = result[high:, :half]
    out_i[3] = result[high:, half:]

    @pl.when(step == STEPS - 1)
    def _():
        texts = emb_t[...].astype(F32)
        grads = acc[...]
        inner = jnp.sum(texts * grads, axis=1, keepdims=True)
        out_t[...] = (scale * (grads - texts * inner)).astype(BF16)
        out_s[...] = jnp.broadcast_to(jnp.sum(sums[...], axis=1, keepdims=True), out_s.shape)


def tile_grads(factors, partner, columns, emb_i, emb_t):
    slabs, high, half = emb_i.shape
    block = slabs // STEPS
    count, width = emb_t.shape
    return pl.pallas_call(
        tile_kernel,
        grid=(STEPS,),
        in_specs=[
            pl.BlockSpec(memory_space=pltpu.SMEM),
            pl.BlockSpec((partner.shape[0] // STEPS, 1), lambda i: (i, 0)),
            pl.BlockSpec((1, count), lambda i: (0, 0)),
            pl.BlockSpec((block, high, half), lambda i: (i, 0, 0)),
            pl.BlockSpec((count, width), lambda i: (0, 0)),
        ],
        out_specs=[
            pl.BlockSpec((block, high, half), lambda i: (i, 0, 0)),
            pl.BlockSpec((count, width), lambda i: (0, 0)),
            pl.BlockSpec((8, 128), lambda i: (0, 0)),
        ],
        out_shape=[
            jax.ShapeDtypeStruct(emb_i.shape, BF16),
            jax.ShapeDtypeStruct(emb_t.shape, BF16),
            jax.ShapeDtypeStruct((8, 128), F32),
        ],
        scratch_shapes=[pltpu.VMEM((count, width), F32), pltpu.VMEM((8, count), F32)],
        compiler_params=pltpu.CompilerParams(vmem_limit_bytes=40 * 1024 * 1024),
    )(factors, partner, columns, emb_i, emb_t)


def half_place(half, j):
    return TEXT_Z + j if half else TEXT_Z - 1 - j


def turn(k):
    return [
        (half_place(half, j), half_place(half, (j + k) % TEXT_Z))
        for half in range(2)
        for j in range(TEXT_Z)
    ]


def finish_kernel(places, first, second, third, fourth, out_i, out_t, rows):
    image_rows = rows.shape[0] // 16
    text_rows = out_t.shape[0] // 64
    padded = first.shape[1] - text_rows
    for k, piece in enumerate((first, second, third, fourth)):
        place = places[k]
        for s in range(16):
            values = piece[s].astype(F32)
            rows[s * image_rows : (s + 1) * image_rows] = values[:image_rows]
            start = pl.multiple_of(place * (16 * text_rows) + s * text_rows, 8)
            out_t[pl.ds(start, text_rows)] = values[padded:]
        start = pl.multiple_of(place * (16 * image_rows), 8)
        out_i[pl.ds(start, 16 * image_rows)] = rows[...]


def finish(places, pieces, image_total, text_total):
    cols = pieces[0].shape[2]
    whole = pl.BlockSpec(memory_space=pltpu.VMEM)
    return pl.pallas_call(
        finish_kernel,
        in_specs=[pl.BlockSpec(memory_space=pltpu.SMEM)] + [whole] * 4,
        out_specs=[whole] * 2,
        out_shape=[
            jax.ShapeDtypeStruct((image_total, cols), F32),
            jax.ShapeDtypeStruct((text_total, cols), F32),
        ],
        scratch_shapes=[pltpu.VMEM((image_total // 4, cols), F32)],
        compiler_params=pltpu.CompilerParams(vmem_limit_bytes=24 * 1024 * 1024),
    )(places, *pieces)


def ring(k):
    return [(i, (i + k) % 4) for i in range(4)]


def y_move(value, k):
    return lax.ppermute(value, ("yl", "yh"), [(i, i ^ k) for i in range(4)])


def pick(value, index, axis=0):
    return lax.dynamic_index_in_dim(value, index, axis, keepdims=False)


def local(
    img_feats, txt_feats, img_gain, txt_gain, img_weight, txt_weight, log_scale, bias, pair_perm
):
    yl, z, x = lax.axis_index("yl"), lax.axis_index("z"), lax.axis_index("x")
    yh, core = lax.axis_index("yh"), lax.axis_index("co")
    pair_count = pair_perm.shape[0]
    img_count, txt_count = img_feats.shape[0], txt_feats.shape[0]
    img_half, txt_half = img_count // 2, txt_count // 2
    piece = txt_half // 4
    is_text = (yl == 1) & (z >= TEXT_Z)
    near = jnp.where(z >= TEXT_Z, z - TEXT_Z, TEXT_Z - 1 - z)
    sources = [jnp.mod(x - k + 4, 4) for k in range(4)]
    targets = [jnp.mod(x + k, 4) for k in range(4)]

    text_hidden = hidden_rows(txt_feats, txt_gain)
    image_hidden = hidden_rows(img_feats, img_gain)
    share_cols = image_hidden.shape[1] // 4
    parts = jnp.stack(
        [image_hidden[:, i * share_cols : (i + 1) * share_cols] for i in range(4)]
    )
    hidden_x = [pick(parts, x)]
    hidden_x += [lax.ppermute(pick(parts, targets[k]), "x", ring(k)) for k in range(1, 4)]

    text_proj = jnp.dot(text_hidden, txt_weight, preferred_element_type=F32)
    image_proj = jnp.dot(image_hidden, img_weight, preferred_element_type=F32)
    squares = jnp.concatenate(
        [jnp.sum(text_proj * text_proj, axis=1), jnp.sum(image_proj * image_proj, axis=1)]
    )
    squares = squares + swap(squares, "co")
    squares = squares + swap(squares, "yh")
    squares, hidden_x[1] = lax.optimization_barrier((squares, hidden_x[1]))
    norms = jnp.sqrt(squares + EPS)[:, None]
    text_norm, image_norm = norms[:txt_count], norms[txt_count:]
    text_emb = (text_proj / text_norm).astype(BF16)
    image_emb = (image_proj / image_norm).astype(BF16)

    def halves(index):
        return jnp.concatenate(
            [
                lax.dynamic_slice_in_dim(image_emb, index * img_half, img_half, 0),
                lax.dynamic_slice_in_dim(text_emb, index * txt_half, txt_half, 0),
            ],
            axis=0,
        )

    kept = halves(core)
    taken = swap(halves(1 - core), "co")
    both = jnp.where(
        core == 0,
        jnp.concatenate([kept, taken], axis=1),
        jnp.concatenate([taken, kept], axis=1),
    )
    width = both.shape[1]
    image_own = both[:img_half]
    text_own = both[img_half:].reshape(4, piece, width)

    got = []
    for k in range(1, 4):
        target = jnp.bitwise_xor(yl * 2 + yh, k)
        got.append(y_move(jnp.concatenate([image_own, pick(text_own, target)], axis=0), k))
    got, hidden_x = lax.optimization_barrier((got, hidden_x))
    slabs = jnp.stack([image_own] + [g[:img_half] for g in got])
    mine = jnp.where(yl == 1, pick(text_own, yl * 2 + yh), got[1][img_half:])
    other = jnp.where(yl == 1, got[0][img_half:], got[2][img_half:])
    chunk = jnp.concatenate([mine, other], axis=1)
    mirror = [(a, Z - 1 - a) for a in range(TEXT_Z, Z)]
    chunk = jnp.where(z >= TEXT_Z, chunk, lax.ppermute(chunk, "z", mirror))
    image_all = jnp.concatenate([slabs] + [lax.ppermute(slabs, "x", ring(k)) for k in range(1, 4)])
    chunks = jnp.stack([chunk] + [lax.ppermute(chunk, "z", turn(k)) for k in range(1, TEXT_Z)])
    text_tile = jnp.stack([chunks, swap(chunks, "co")])
    text_tile = text_tile.reshape(2 * TEXT_Z * piece, 2 * width)

    quarter = yl * 2 + yh
    order = jnp.arange(TEXT_Z, dtype=jnp.int32)
    group = jnp.mod(near - order + TEXT_Z, TEXT_Z) * 4 + x
    columns = (
        group[None, :, None] * txt_count
        + jnp.mod(core + jnp.arange(2, dtype=jnp.int32), 2)[:, None, None] * txt_half
        + quarter * piece
        + jnp.arange(piece, dtype=jnp.int32)[None, None, :]
    ).reshape(1, -1)
    padded = jnp.concatenate([pair_perm, jnp.full((16 * img_count,), -1, jnp.int32)])
    padded = pick(pick(padded.reshape(2, Z, 4, 2, img_half), z, 1), core, 2)
    padded = jnp.where(yl == 0, padded, padded[::-1])
    partner = jnp.stack([pick(padded, source, 1) for source in sources]).reshape(-1, 1)
    logit_scale = jnp.exp(log_scale[0])
    weights = [
        jnp.where((side == 1) & (z >= TEXT_Z), 0.0, 1.0).astype(F32) for side in (yl, 1 - yl)
    ]
    factors = jnp.stack([logit_scale, bias[0], *weights])

    image_part, text_part, part_sums = tile_grads(factors, partner, columns, image_all, text_tile)

    text_part = text_part.reshape(2, TEXT_Z, piece, 2 * width)
    both = text_part[0].astype(F32) + swap(text_part[1], "co").astype(F32)
    rounded = both.astype(BF16)
    image_part = image_part.reshape(4, 4, img_half, width)
    text_got = [lax.ppermute(rounded[k], "z", turn(TEXT_Z - k)) for k in range(1, TEXT_Z)]
    image_near = [lax.ppermute(image_part[k], "x", ring(-k)) for k in (1, 3)]
    text_got[:2], image_far = lax.optimization_barrier((text_got[:2], image_part[2]))
    image_far = lax.ppermute(image_far, "x", ring(-2))
    text_got, image_near, image_far = lax.optimization_barrier((text_got, image_near, image_far))
    text_sum = both[0]
    for g in text_got:
        text_sum = text_sum + g.astype(F32)
    text_round = text_sum.astype(BF16)
    image_sum = image_part[0].astype(F32)
    for g in (*image_near, image_far):
        image_sum = image_sum + g.astype(F32)

    text_round, image_round = lax.optimization_barrier((text_round, image_sum.astype(BF16)))
    image_sum = image_sum[0]
    for k in range(1, 4):
        image_sum = image_sum + y_move(image_round[k], k).astype(F32)
    text_mirror = lax.ppermute(text_round, "z", [(b, a) for a, b in mirror])
    text_sum, text_mirror, image_sum = lax.optimization_barrier(
        (text_sum, text_mirror, image_sum)
    )
    text_sum = (text_sum + text_mirror.astype(F32)).astype(BF16)
    same, cross = text_sum[:, :width], text_sum[:, width:]
    across, straight, diagonal = [y_move(cross if k & 1 else same, k) for k in range(1, 4)]
    cols = width // 2

    def join_cores(rows):
        kept = lax.dynamic_slice_in_dim(rows, core * cols, cols, 1)
        taken = swap(lax.dynamic_slice_in_dim(rows, (1 - core) * cols, cols, 1), "co")
        return jnp.where(
            core == 0,
            jnp.concatenate([kept, taken], axis=0),
            jnp.concatenate([taken, kept], axis=0),
        )

    image_rows = image_sum / lax.dynamic_slice_in_dim(image_norm, core * img_half, img_half, 0)
    image_du = join_cores(image_rows.astype(BF16))
    straight, image_du = lax.optimization_barrier((straight, image_du))
    du_x = [image_du] + [lax.ppermute(image_du, "x", ring(k)) for k in range(1, 4)]
    transposed = (((0,), (0,)), ((), ()))

    text_rows = jnp.where(
        yh == 0,
        jnp.concatenate([straight, diagonal, same, across], axis=0),
        jnp.concatenate([diagonal, straight, across, same], axis=0),
    )
    text_rows = text_rows.astype(F32) / lax.dynamic_slice_in_dim(
        text_norm, core * txt_half, txt_half, 0
    )
    text_du = join_cores(jnp.where(is_text, text_rows, 0.0).astype(BF16))
    text_weight = lax.dot_general(text_hidden, text_du, transposed, preferred_element_type=F32)
    image_weight = lax.dot_general(
        jnp.concatenate(hidden_x), jnp.concatenate(du_x), transposed, preferred_element_type=F32
    )
    text_share = text_weight.shape[0] // 4
    img_share, txt_share = share_cols // 16, text_share // 16
    own_weight = lax.dynamic_slice_in_dim(img_weight, x * share_cols, share_cols, 0)
    own_gain = lax.dynamic_slice_in_dim(img_gain, x * share_cols, share_cols, 0)
    small = jnp.concatenate(
        [
            jnp.sum(image_weight * own_weight.astype(F32), axis=1) / own_gain,
            jnp.sum(text_weight * txt_weight.astype(F32), axis=1) / txt_gain,
            part_sums[:3, 0],
        ]
    )
    small = small + swap(small, "co")
    small = small + swap(small, "yh")

    text_weight = text_weight.reshape(4, text_share, cols)
    got = [
        lax.ppermute(pick(text_weight, targets[k]).astype(BF16), "x", ring(k)) for k in range(1, 4)
    ]
    text_weight = pick(text_weight, x)
    for g in got:
        text_weight = text_weight + g.astype(F32)

    slot = 32
    spare = slot - img_share
    used = img_share + 4 * txt_share

    def spare_rows(values):
        rows = jnp.stack(split3(values), axis=1)
        return jnp.pad(rows, ((0, 0), (0, spare - 3), (0, cols - values.shape[1])))

    def joined(blocks):
        rows = blocks[..., img_share:slot, :].astype(F32)
        return rows[..., 0, :] + rows[..., 1, :] + rows[..., 2, :]

    sums = jnp.broadcast_to(small[None, share_cols + 4 * text_share :], (16, 3))
    vector = jnp.concatenate(
        [
            small[:share_cols].reshape(16, img_share),
            small[share_cols : share_cols + 4 * text_share].reshape(16, 4 * txt_share),
            sums,
        ],
        axis=1,
    )
    block = jnp.concatenate(
        [
            image_weight.astype(BF16).reshape(16, img_share, cols),
            spare_rows(vector),
            text_weight.astype(BF16).reshape(16, txt_share, cols),
        ],
        axis=1,
    )
    reduced = exchange(block, ("yl", "z"))
    vector = jnp.sum(joined(reduced), axis=0)
    reduced = jnp.sum(reduced.astype(F32), axis=0)
    ready = jnp.concatenate(
        [
            reduced[:img_share].astype(BF16),
            spare_rows(vector[None, : used + 3])[0],
            reduced[slot:].astype(BF16),
        ],
        axis=0,
    )
    gathered = exchange(jnp.broadcast_to(ready, (16, *ready.shape)), ("yl", "z"))
    pieces = [gathered] + [lax.ppermute(gathered, "x", ring(k)) for k in range(1, 4)]
    image_grad, text_grad = finish(
        jnp.stack(sources), pieces, img_weight.shape[0], txt_weight.shape[0]
    )
    vectors = jnp.stack([joined(piece) for piece in pieces])
    total = jnp.sum(vectors[:, :, img_share : used + 3], axis=0)
    gains = jnp.stack([pick(vectors, jnp.mod(x - a + 4, 4)) for a in range(4)])
    loss_parts = total[0, 4 * txt_share :]
    return (
        loss_parts[0:1] / pair_count,
        image_grad,
        text_grad,
        gains[:, :, :img_share].reshape(-1),
        total[:, : 4 * txt_share].reshape(-1),
        loss_parts[1:2] * logit_scale,
        loss_parts[2:3],
    )


def solution(mesh):
    inner = Mesh(mesh.devices.reshape(2, Z, 4, 2, 2), ("yl", "z", "x", "yh", "co"))
    tensor = ("yh", "co")
    return jax.shard_map(
        local,
        mesh=inner,
        in_specs=(
            P(DP, None),
            P(DP, None),
            P(),
            P(),
            P(None, tensor),
            P(None, tensor),
            P(),
            P(),
            P(),
        ),
        out_specs=(P(), P(None, tensor), P(None, tensor), P(), P(), P(), P()),
        check_vma=False,
    )
```

```python
import jax
import jax.numpy as jnp
from jax import lax
from jax.experimental import pallas as pl
from jax.experimental.pallas import tpu as pltpu
from jax.sharding import Mesh, PartitionSpec as P

EPS = 1e-06
F32 = jnp.float32
BF16 = jnp.bfloat16
Z = 8
TEXT_Z = 4
DP = ("yl", "z", "x")


def hidden_rows(features, gain_vec):
    values = features.astype(F32)
    center = jnp.mean(values, axis=1, keepdims=True)
    spread = jnp.mean(values * values, axis=1, keepdims=True) - center * center
    scaled = (values - center) * lax.rsqrt(spread + EPS)
    return (scaled * gain_vec).astype(BF16)


def swap(value, axis):
    return lax.ppermute(value, axis, [(0, 1), (1, 0)])


def exchange(value, axes):
    return lax.all_to_all(value, axes, split_axis=0, concat_axis=0, tiled=True)


def split3(value):
    high = value.astype(BF16)
    rest = value - high.astype(F32)
    middle = rest.astype(BF16)
    return high, middle, (rest - middle.astype(F32)).astype(BF16)


def tile_rows(emb_i, i):
    base = 4 * i
    return jnp.concatenate(
        [
            jnp.concatenate([emb_i[base], emb_i[base + 1]], axis=1),
            jnp.concatenate([emb_i[base + 2], emb_i[base + 3]], axis=1),
        ],
        axis=0,
    )


def tile_kernel(
    factors, partner, columns, emb_i, emb_t, out_i, out_t, out_s, acc, sums
):
    scale, shift = factors[0], factors[1]
    high, half = emb_i.shape[1], emb_i.shape[2]
    place = lax.broadcasted_iota(jnp.int32, (2 * high, 1), 0)
    weight = jnp.where(place < high, factors[2], factors[3])
    nt = (((1,), (1,)), ((), ()))
    tn = (((0,), (0,)), ((), ()))

    def grads(similar, i):
        logits = scale * similar + shift
        pair = partner[2 * high * i : 2 * high * (i + 1)] == columns[...]
        signed = jnp.where(pair, -logits, logits)
        small = jnp.exp(-jnp.abs(signed))
        total = 1.0 + small
        inverse = 1.0 / total
        sigmoid = jnp.where(signed >= 0, inverse, small * inverse)
        soft = jnp.maximum(signed, 0.0) + jnp.log(total) + (small - (total - 1.0)) * inverse
        grad = jnp.where(pair, -sigmoid, sigmoid) * weight
        parts = [
            jnp.sum(soft * weight, axis=0, keepdims=True),
            jnp.sum(grad * similar, axis=0, keepdims=True),
            jnp.sum(grad, axis=0, keepdims=True),
        ]
        for j, part in enumerate(parts):
            if i == 0:
                sums[j : j + 1] = part
            else:
                sums[j : j + 1] += part
        return grad.astype(BF16)

    def finish_rows(rounded, rows, i):
        update = lax.dot_general(rounded, rows, tn, preferred_element_type=F32)
        if i == 0:
            acc[...] = update
        else:
            acc[...] += update
        grad_rows = jnp.dot(rounded, emb_t[...], preferred_element_type=F32)
        wide = rows.astype(F32)
        inner = jnp.sum(wide * grad_rows, axis=1, keepdims=True)
        result = (scale * (grad_rows - wide * inner)).astype(BF16)
        out_i[4 * i] = result[:high, :half]
        out_i[4 * i + 1] = result[:high, half:]
        out_i[4 * i + 2] = result[high:, :half]
        out_i[4 * i + 3] = result[high:, half:]

    rows = tile_rows(emb_i, 0)
    similar = lax.dot_general(rows, emb_t[...], nt, preferred_element_type=F32)
    for i in range(4):
        if i < 3:
            later = tile_rows(emb_i, i + 1)
            ahead = lax.dot_general(later, emb_t[...], nt, preferred_element_type=F32)
        rounded = grads(similar, i)
        finish_rows(rounded, rows, i)
        if i < 3:
            rows, similar = later, ahead
    sums[3:] = jnp.zeros_like(sums[3:])
    texts = emb_t[...].astype(F32)
    grads_t = acc[...]
    inner = jnp.sum(texts * grads_t, axis=1, keepdims=True)
    out_t[...] = (scale * (grads_t - texts * inner)).astype(BF16)
    out_s[...] = jnp.broadcast_to(jnp.sum(sums[...], axis=1, keepdims=True), out_s.shape)


def tile_grads(factors, partner, columns, emb_i, emb_t):
    count, width = emb_t.shape
    whole = pl.BlockSpec(memory_space=pltpu.VMEM)
    return pl.pallas_call(
        tile_kernel,
        in_specs=[pl.BlockSpec(memory_space=pltpu.SMEM)] + [whole] * 4,
        out_specs=[whole] * 3,
        out_shape=[
            jax.ShapeDtypeStruct(emb_i.shape, BF16),
            jax.ShapeDtypeStruct(emb_t.shape, BF16),
            jax.ShapeDtypeStruct((8, 128), F32),
        ],
        scratch_shapes=[pltpu.VMEM((count, width), F32), pltpu.VMEM((8, count), F32)],
        compiler_params=pltpu.CompilerParams(vmem_limit_bytes=40 * 1024 * 1024),
    )(factors, partner, columns, emb_i, emb_t)


def half_place(half, j):
    return TEXT_Z + j if half else TEXT_Z - 1 - j


def turn(k):
    return [
        (half_place(half, j), half_place(half, (j + k) % TEXT_Z))
        for half in range(2)
        for j in range(TEXT_Z)
    ]


def finish_kernel(places, first, second, third, fourth, out_i, out_t, out_g, rows):
    image_rows = rows.shape[0] // 16
    text_rows = out_t.shape[0] // 64
    padded = first.shape[1] - text_rows
    for k, piece in enumerate((first, second, third, fourth)):
        place = places[k]
        for s in range(16):
            values = piece[s].astype(F32)
            rows[s * image_rows : (s + 1) * image_rows] = values[:image_rows]
            start = pl.multiple_of(place * (16 * text_rows) + s * text_rows, 8)
            out_t[pl.ds(start, text_rows)] = values[padded:]
            tail = values[image_rows:padded]
            out_g[place, s : s + 1] = tail[0:1] + tail[1:2] + tail[2:3]
        start = pl.multiple_of(place * (16 * image_rows), 8)
        out_i[pl.ds(start, 16 * image_rows)] = rows[...]


def finish(places, pieces, image_total, text_total):
    cols = pieces[0].shape[2]
    whole = pl.BlockSpec(memory_space=pltpu.VMEM)
    return pl.pallas_call(
        finish_kernel,
        in_specs=[pl.BlockSpec(memory_space=pltpu.SMEM)] + [whole] * 4,
        out_specs=[whole] * 3,
        out_shape=[
            jax.ShapeDtypeStruct((image_total, cols), F32),
            jax.ShapeDtypeStruct((text_total, cols), F32),
            jax.ShapeDtypeStruct((4, 16, cols), F32),
        ],
        scratch_shapes=[pltpu.VMEM((image_total // 4, cols), F32)],
        compiler_params=pltpu.CompilerParams(vmem_limit_bytes=24 * 1024 * 1024),
    )(places, *pieces)


def ring(k):
    return [(i, (i + k) % 4) for i in range(4)]


def y_move(value, k):
    return lax.ppermute(value, ("yl", "yh"), [(i, i ^ k) for i in range(4)])


def pick(value, index, axis=0):
    return lax.dynamic_index_in_dim(value, index, axis, keepdims=False)


def local(
    img_feats, txt_feats, img_gain, txt_gain, img_weight, txt_weight, log_scale, bias, pair_perm
):
    yl, z, x = lax.axis_index("yl"), lax.axis_index("z"), lax.axis_index("x")
    yh, core = lax.axis_index("yh"), lax.axis_index("co")
    pair_count = pair_perm.shape[0]
    img_count, txt_count = img_feats.shape[0], txt_feats.shape[0]
    img_half, txt_half = img_count // 2, txt_count // 2
    piece = txt_half // 4
    is_text = (yl == 1) & (z >= TEXT_Z)
    near = jnp.where(z >= TEXT_Z, z - TEXT_Z, TEXT_Z - 1 - z)
    sources = [jnp.mod(x - k + 4, 4) for k in range(4)]
    targets = [jnp.mod(x + k, 4) for k in range(4)]

    text_hidden = hidden_rows(txt_feats, txt_gain)
    image_hidden = hidden_rows(img_feats, img_gain)
    share_cols = image_hidden.shape[1] // 4
    parts = jnp.stack(
        [image_hidden[:, i * share_cols : (i + 1) * share_cols] for i in range(4)]
    )
    hidden_x = [pick(parts, x)]
    hidden_x += [lax.ppermute(pick(parts, targets[k]), "x", ring(k)) for k in range(1, 4)]

    text_proj = jnp.dot(text_hidden, txt_weight, preferred_element_type=F32)
    image_proj = jnp.dot(image_hidden, img_weight, preferred_element_type=F32)
    squares = jnp.concatenate(
        [jnp.sum(text_proj * text_proj, axis=1), jnp.sum(image_proj * image_proj, axis=1)]
    )
    squares = squares + swap(squares, "co")
    squares = squares + swap(squares, "yh")
    squares, hidden_x[1] = lax.optimization_barrier((squares, hidden_x[1]))
    norms = jnp.sqrt(squares + EPS)[:, None]
    text_norm, image_norm = norms[:txt_count], norms[txt_count:]
    text_emb = (text_proj / text_norm).astype(BF16)
    image_emb = (image_proj / image_norm).astype(BF16)

    def halves(index):
        return jnp.concatenate(
            [
                lax.dynamic_slice_in_dim(image_emb, index * img_half, img_half, 0),
                lax.dynamic_slice_in_dim(text_emb, index * txt_half, txt_half, 0),
            ],
            axis=0,
        )

    kept = halves(core)
    taken = swap(halves(1 - core), "co")
    both = jnp.where(
        core == 0,
        jnp.concatenate([kept, taken], axis=1),
        jnp.concatenate([taken, kept], axis=1),
    )
    width = both.shape[1]
    image_own = both[:img_half]
    text_own = both[img_half:].reshape(4, piece, width)

    got = []
    for k in range(1, 4):
        target = jnp.bitwise_xor(yl * 2 + yh, k)
        got.append(y_move(jnp.concatenate([image_own, pick(text_own, target)], axis=0), k))
    got, hidden_x = lax.optimization_barrier((got, hidden_x))
    slabs = jnp.stack([image_own] + [g[:img_half] for g in got])
    mine = jnp.where(yl == 1, pick(text_own, yl * 2 + yh), got[1][img_half:])
    other = jnp.where(yl == 1, got[0][img_half:], got[2][img_half:])
    chunk = jnp.concatenate([mine, other], axis=1)
    mirror = [(a, Z - 1 - a) for a in range(TEXT_Z, Z)]
    chunk = jnp.where(z >= TEXT_Z, chunk, lax.ppermute(chunk, "z", mirror))
    image_all = jnp.concatenate([slabs] + [lax.ppermute(slabs, "x", ring(k)) for k in range(1, 4)])
    chunks = jnp.stack([chunk] + [lax.ppermute(chunk, "z", turn(k)) for k in range(1, TEXT_Z)])
    text_tile = jnp.stack([chunks, swap(chunks, "co")])
    text_tile = text_tile.reshape(2 * TEXT_Z * piece, 2 * width)

    quarter = yl * 2 + yh
    order = jnp.arange(TEXT_Z, dtype=jnp.int32)
    group = jnp.mod(near - order + TEXT_Z, TEXT_Z) * 4 + x
    columns = (
        group[None, :, None] * txt_count
        + jnp.mod(core + jnp.arange(2, dtype=jnp.int32), 2)[:, None, None] * txt_half
        + quarter * piece
        + jnp.arange(piece, dtype=jnp.int32)[None, None, :]
    ).reshape(1, -1)
    padded = jnp.concatenate([pair_perm, jnp.full((16 * img_count,), -1, jnp.int32)])
    padded = pick(pick(padded.reshape(2, Z, 4, 2, img_half), z, 1), core, 2)
    padded = jnp.where(yl == 0, padded, padded[::-1])
    partner = jnp.stack([pick(padded, source, 1) for source in sources]).reshape(-1, 1)
    logit_scale = jnp.exp(log_scale[0])
    weights = [
        jnp.where((side == 1) & (z >= TEXT_Z), 0.0, 1.0).astype(F32) for side in (yl, 1 - yl)
    ]
    factors = jnp.stack([logit_scale, bias[0], *weights])

    image_part, text_part, part_sums = tile_grads(factors, partner, columns, image_all, text_tile)

    text_part = text_part.reshape(2, TEXT_Z, piece, 2 * width)
    both = text_part[0].astype(F32) + swap(text_part[1], "co").astype(F32)
    rounded = both.astype(BF16)
    image_part = image_part.reshape(4, 4, img_half, width)
    text_got = [lax.ppermute(rounded[k], "z", turn(TEXT_Z - k)) for k in range(1, TEXT_Z)]
    image_near = [lax.ppermute(image_part[k], "x", ring(-k)) for k in (1, 3)]
    text_got[:2], image_far = lax.optimization_barrier((text_got[:2], image_part[2]))
    image_far = lax.ppermute(image_far, "x", ring(-2))
    text_got, image_near, image_far = lax.optimization_barrier((text_got, image_near, image_far))
    text_sum = both[0]
    for g in text_got:
        text_sum = text_sum + g.astype(F32)
    text_round = text_sum.astype(BF16)
    image_sum = image_part[0].astype(F32)
    for g in (*image_near, image_far):
        image_sum = image_sum + g.astype(F32)

    text_round, image_round = lax.optimization_barrier((text_round, image_sum.astype(BF16)))
    image_sum = image_sum[0]
    for k in range(1, 4):
        image_sum = image_sum + y_move(image_round[k], k).astype(F32)
    text_mirror = lax.ppermute(text_round, "z", [(b, a) for a, b in mirror])
    text_sum, text_mirror, image_sum = lax.optimization_barrier(
        (text_sum, text_mirror, image_sum)
    )
    text_sum = (text_sum + text_mirror.astype(F32)).astype(BF16)
    same, cross = text_sum[:, :width], text_sum[:, width:]
    across, straight, diagonal = [y_move(cross if k & 1 else same, k) for k in range(1, 4)]
    cols = width // 2

    def join_cores(rows):
        kept = lax.dynamic_slice_in_dim(rows, core * cols, cols, 1)
        taken = swap(lax.dynamic_slice_in_dim(rows, (1 - core) * cols, cols, 1), "co")
        return jnp.where(
            core == 0,
            jnp.concatenate([kept, taken], axis=0),
            jnp.concatenate([taken, kept], axis=0),
        )

    image_rows = image_sum / lax.dynamic_slice_in_dim(image_norm, core * img_half, img_half, 0)
    image_du = join_cores(image_rows.astype(BF16))
    straight, image_du = lax.optimization_barrier((straight, image_du))
    du_x = [image_du] + [lax.ppermute(image_du, "x", ring(k)) for k in range(1, 4)]
    transposed = (((0,), (0,)), ((), ()))

    text_rows = jnp.where(
        yh == 0,
        jnp.concatenate([straight, diagonal, same, across], axis=0),
        jnp.concatenate([diagonal, straight, across, same], axis=0),
    )
    text_rows = text_rows.astype(F32) / lax.dynamic_slice_in_dim(
        text_norm, core * txt_half, txt_half, 0
    )
    text_du = join_cores(jnp.where(is_text, text_rows, 0.0).astype(BF16))
    text_weight = lax.dot_general(text_hidden, text_du, transposed, preferred_element_type=F32)
    text_share = text_weight.shape[0] // 4
    text_whole = text_weight
    text_weight = text_weight.reshape(4, text_share, cols)
    got = [
        lax.ppermute(pick(text_weight, targets[k]).astype(BF16), "x", ring(k)) for k in range(1, 4)
    ]
    got[0], du_x = lax.optimization_barrier((got[0], du_x))
    image_weight = lax.dot_general(
        jnp.concatenate(hidden_x), jnp.concatenate(du_x), transposed, preferred_element_type=F32
    )
    img_share, txt_share = share_cols // 16, text_share // 16
    own_weight = lax.dynamic_slice_in_dim(img_weight, x * share_cols, share_cols, 0)
    own_gain = lax.dynamic_slice_in_dim(img_gain, x * share_cols, share_cols, 0)
    small = jnp.concatenate(
        [
            jnp.sum(image_weight * own_weight.astype(F32), axis=1) / own_gain,
            jnp.sum(text_whole * txt_weight.astype(F32), axis=1) / txt_gain,
            part_sums[:3, 0],
        ]
    )
    small = small + swap(small, "co")
    small = small + swap(small, "yh")
    text_weight = pick(text_weight, x)
    for g in got:
        text_weight = text_weight + g.astype(F32)

    slot = 32
    spare = slot - img_share
    used = img_share + 4 * txt_share

    def spare_rows(values):
        rows = jnp.stack(split3(values), axis=1)
        return jnp.pad(rows, ((0, 0), (0, spare - 3), (0, cols - values.shape[1])))

    def joined(blocks):
        rows = blocks[..., img_share:slot, :].astype(F32)
        return rows[..., 0, :] + rows[..., 1, :] + rows[..., 2, :]

    sums = jnp.broadcast_to(small[None, share_cols + 4 * text_share :], (16, 3))
    vector = jnp.concatenate(
        [
            small[:share_cols].reshape(16, img_share),
            small[share_cols : share_cols + 4 * text_share].reshape(16, 4 * txt_share),
            sums,
        ],
        axis=1,
    )
    block = jnp.concatenate(
        [
            image_weight.astype(BF16).reshape(16, img_share, cols),
            spare_rows(vector),
            text_weight.astype(BF16).reshape(16, txt_share, cols),
        ],
        axis=1,
    )
    reduced = exchange(block, ("yl", "z"))
    vector = jnp.sum(joined(reduced), axis=0)
    reduced = jnp.sum(reduced.astype(F32), axis=0)
    ready = jnp.concatenate(
        [
            reduced[:img_share].astype(BF16),
            spare_rows(vector[None, : used + 3])[0],
            reduced[slot:].astype(BF16),
        ],
        axis=0,
    )
    gathered = exchange(jnp.broadcast_to(ready, (16, *ready.shape)), ("yl", "z"))
    pieces = [gathered] + [lax.ppermute(gathered, "x", ring(k)) for k in range(1, 4)]
    image_grad, text_grad, vectors = finish(
        jnp.stack(sources), pieces, img_weight.shape[0], txt_weight.shape[0]
    )
    total = jnp.sum(vectors[:, :, img_share : used + 3], axis=0)
    loss_parts = total[0, 4 * txt_share :]
    return (
        loss_parts[0:1] / pair_count,
        image_grad,
        text_grad,
        vectors[:, :, :img_share].reshape(-1),
        total[:, : 4 * txt_share].reshape(-1),
        loss_parts[1:2] * logit_scale,
        loss_parts[2:3],
    )


def solution(mesh):
    inner = Mesh(mesh.devices.reshape(2, Z, 4, 2, 2), ("yl", "z", "x", "yh", "co"))
    tensor = ("yh", "co")
    return jax.shard_map(
        local,
        mesh=inner,
        in_specs=(
            P(DP, None),
            P(DP, None),
            P(),
            P(),
            P(None, tensor),
            P(None, tensor),
            P(),
            P(),
            P(),
        ),
        out_specs=(P(), P(None, tensor), P(None, tensor), P(), P(), P(), P()),
        check_vma=False,
    )
```

```python
import jax
import jax.numpy as jnp
from jax import lax
from jax.experimental import pallas as pl
from jax.experimental.pallas import tpu as pltpu
from jax.sharding import Mesh, PartitionSpec as P

EPS = 1e-06
F32 = jnp.float32
BF16 = jnp.bfloat16
Z = 8
TEXT_Z = 4
DP = ("yl", "z", "x")


def hidden_rows(features, gain_vec):
    values = features.astype(F32)
    center = jnp.mean(values, axis=1, keepdims=True)
    spread = jnp.mean(values * values, axis=1, keepdims=True) - center * center
    scaled = (values - center) * lax.rsqrt(spread + EPS)
    return (scaled * gain_vec).astype(BF16)


def swap(value, axis):
    return lax.ppermute(value, axis, [(0, 1), (1, 0)])


def exchange(value, axes):
    return lax.all_to_all(value, axes, split_axis=0, concat_axis=0, tiled=True)


def split3(value):
    high = value.astype(BF16)
    rest = value - high.astype(F32)
    middle = rest.astype(BF16)
    return high, middle, (rest - middle.astype(F32)).astype(BF16)


def tile_rows(emb_i, i):
    base = 4 * i
    return jnp.concatenate(
        [
            jnp.concatenate([emb_i[base], emb_i[base + 1]], axis=1),
            jnp.concatenate([emb_i[base + 2], emb_i[base + 3]], axis=1),
        ],
        axis=0,
    )


def tile_kernel(
    factors, partner, columns, emb_i, emb_t, out_i, out_t, out_s, acc, sums
):
    scale, shift = factors[0], factors[1]
    high, half = emb_i.shape[1], emb_i.shape[2]
    place = lax.broadcasted_iota(jnp.int32, (2 * high, 1), 0)
    weight = jnp.where(place < high, factors[2], factors[3])
    nt = (((1,), (1,)), ((), ()))
    tn = (((0,), (0,)), ((), ()))

    def grads(similar, i):
        logits = scale * similar + shift
        pair = partner[2 * high * i : 2 * high * (i + 1)] == columns[...]
        signed = jnp.where(pair, -logits, logits)
        small = jnp.exp(-jnp.abs(signed))
        total = 1.0 + small
        inverse = 1.0 / total
        sigmoid = jnp.where(signed >= 0, inverse, small * inverse)
        soft = jnp.maximum(signed, 0.0) + jnp.log(total) + (small - (total - 1.0)) * inverse
        grad = jnp.where(pair, -sigmoid, sigmoid) * weight
        parts = [
            jnp.sum(soft * weight, axis=0, keepdims=True),
            jnp.sum(grad * similar, axis=0, keepdims=True),
            jnp.sum(grad, axis=0, keepdims=True),
        ]
        for j, part in enumerate(parts):
            if i == 0:
                sums[j : j + 1] = part
            else:
                sums[j : j + 1] += part
        return grad.astype(BF16)

    def finish_rows(rounded, rows, i):
        update = lax.dot_general(rounded, rows, tn, preferred_element_type=F32)
        if i == 0:
            acc[...] = update
        else:
            acc[...] += update
        grad_rows = jnp.dot(rounded, emb_t[...], preferred_element_type=F32)
        wide = rows.astype(F32)
        inner = jnp.sum(wide * grad_rows, axis=1, keepdims=True)
        result = (scale * (grad_rows - wide * inner)).astype(BF16)
        out_i[4 * i] = result[:high, :half]
        out_i[4 * i + 1] = result[:high, half:]
        out_i[4 * i + 2] = result[high:, :half]
        out_i[4 * i + 3] = result[high:, half:]

    rows = tile_rows(emb_i, 0)
    similar = lax.dot_general(rows, emb_t[...], nt, preferred_element_type=F32)
    for i in range(4):
        if i < 3:
            later = tile_rows(emb_i, i + 1)
            ahead = lax.dot_general(later, emb_t[...], nt, preferred_element_type=F32)
        rounded = grads(similar, i)
        finish_rows(rounded, rows, i)
        if i < 3:
            rows, similar = later, ahead
    sums[3:] = jnp.zeros_like(sums[3:])
    texts = emb_t[...].astype(F32)
    grads_t = acc[...]
    inner = jnp.sum(texts * grads_t, axis=1, keepdims=True)
    out_t[...] = (scale * (grads_t - texts * inner)).astype(BF16)
    out_s[...] = jnp.broadcast_to(jnp.sum(sums[...], axis=1, keepdims=True), out_s.shape)


def tile_grads(factors, partner, columns, emb_i, emb_t):
    count, width = emb_t.shape
    whole = pl.BlockSpec(memory_space=pltpu.VMEM)
    return pl.pallas_call(
        tile_kernel,
        in_specs=[pl.BlockSpec(memory_space=pltpu.SMEM)] + [whole] * 4,
        out_specs=[whole] * 3,
        out_shape=[
            jax.ShapeDtypeStruct(emb_i.shape, BF16),
            jax.ShapeDtypeStruct(emb_t.shape, BF16),
            jax.ShapeDtypeStruct((8, 128), F32),
        ],
        scratch_shapes=[pltpu.VMEM((count, width), F32), pltpu.VMEM((8, count), F32)],
        compiler_params=pltpu.CompilerParams(vmem_limit_bytes=40 * 1024 * 1024),
    )(factors, partner, columns, emb_i, emb_t)


def half_place(half, j):
    return TEXT_Z + j if half else TEXT_Z - 1 - j


def turn(k):
    return [
        (half_place(half, j), half_place(half, (j + k) % TEXT_Z))
        for half in range(2)
        for j in range(TEXT_Z)
    ]


def finish_kernel(places, first, second, third, fourth, out_i, out_t, out_g, rows):
    image_rows = rows.shape[0] // 16
    text_rows = out_t.shape[0] // 64
    padded = first.shape[1] - text_rows
    for k, piece in enumerate((first, second, third, fourth)):
        place = places[k]
        for s in range(16):
            values = piece[s].astype(F32)
            rows[s * image_rows : (s + 1) * image_rows] = values[:image_rows]
            start = pl.multiple_of(place * (16 * text_rows) + s * text_rows, 8)
            out_t[pl.ds(start, text_rows)] = values[padded:]
            tail = values[image_rows:padded]
            out_g[place, s : s + 1] = tail[0:1] + tail[1:2] + tail[2:3]
        start = pl.multiple_of(place * (16 * image_rows), 8)
        out_i[pl.ds(start, 16 * image_rows)] = rows[...]


def finish(places, pieces, image_total, text_total):
    cols = pieces[0].shape[2]
    whole = pl.BlockSpec(memory_space=pltpu.VMEM)
    return pl.pallas_call(
        finish_kernel,
        in_specs=[pl.BlockSpec(memory_space=pltpu.SMEM)] + [whole] * 4,
        out_specs=[whole] * 3,
        out_shape=[
            jax.ShapeDtypeStruct((image_total, cols), F32),
            jax.ShapeDtypeStruct((text_total, cols), F32),
            jax.ShapeDtypeStruct((4, 16, cols), F32),
        ],
        scratch_shapes=[pltpu.VMEM((image_total // 4, cols), F32)],
        compiler_params=pltpu.CompilerParams(vmem_limit_bytes=24 * 1024 * 1024),
    )(places, *pieces)


def ring(k):
    return [(i, (i + k) % 4) for i in range(4)]


def y_move(value, k):
    return lax.ppermute(value, ("yl", "yh"), [(i, i ^ k) for i in range(4)])


def pick(value, index, axis=0):
    return lax.dynamic_index_in_dim(value, index, axis, keepdims=False)


def local(
    img_feats, txt_feats, img_gain, txt_gain, img_weight, txt_weight, log_scale, bias, pair_perm
):
    yl, z, x = lax.axis_index("yl"), lax.axis_index("z"), lax.axis_index("x")
    yh, core = lax.axis_index("yh"), lax.axis_index("co")
    pair_count = pair_perm.shape[0]
    img_count, txt_count = img_feats.shape[0], txt_feats.shape[0]
    img_half, txt_half = img_count // 2, txt_count // 2
    piece = txt_half // 4
    is_text = (yl == 1) & (z >= TEXT_Z)
    near = jnp.where(z >= TEXT_Z, z - TEXT_Z, TEXT_Z - 1 - z)
    sources = [jnp.mod(x - k + 4, 4) for k in range(4)]
    targets = [jnp.mod(x + k, 4) for k in range(4)]

    image_hidden = hidden_rows(img_feats, img_gain)
    image_hidden, text_gain = lax.optimization_barrier((image_hidden, txt_gain))
    text_hidden = hidden_rows(txt_feats, text_gain)
    share_cols = image_hidden.shape[1] // 4
    parts = jnp.stack(
        [image_hidden[:, i * share_cols : (i + 1) * share_cols] for i in range(4)]
    )
    hidden_x = [pick(parts, x)]
    hidden_x += [lax.ppermute(pick(parts, targets[k]), "x", ring(k)) for k in range(1, 4)]

    text_proj = jnp.dot(text_hidden, txt_weight, preferred_element_type=F32)
    image_proj = jnp.dot(image_hidden, img_weight, preferred_element_type=F32)
    squares = jnp.concatenate(
        [jnp.sum(text_proj * text_proj, axis=1), jnp.sum(image_proj * image_proj, axis=1)]
    )
    squares = squares + swap(squares, "co")
    squares = squares + swap(squares, "yh")
    norms = jnp.sqrt(squares + EPS)[:, None]
    text_norm, image_norm = norms[:txt_count], norms[txt_count:]
    text_emb = (text_proj / text_norm).astype(BF16)
    image_emb = (image_proj / image_norm).astype(BF16)

    def halves(index):
        return jnp.concatenate(
            [
                lax.dynamic_slice_in_dim(image_emb, index * img_half, img_half, 0),
                lax.dynamic_slice_in_dim(text_emb, index * txt_half, txt_half, 0),
            ],
            axis=0,
        )

    kept = halves(core)
    taken = swap(halves(1 - core), "co")
    both = jnp.where(
        core == 0,
        jnp.concatenate([kept, taken], axis=1),
        jnp.concatenate([taken, kept], axis=1),
    )
    width = both.shape[1]
    image_own = both[:img_half]
    text_own = both[img_half:].reshape(4, piece, width)

    got = []
    for k in range(1, 4):
        target = jnp.bitwise_xor(yl * 2 + yh, k)
        got.append(y_move(jnp.concatenate([image_own, pick(text_own, target)], axis=0), k))
    got, hidden_x = lax.optimization_barrier((got, hidden_x))
    slabs = jnp.stack([image_own] + [g[:img_half] for g in got])
    mine = jnp.where(yl == 1, pick(text_own, yl * 2 + yh), got[1][img_half:])
    other = jnp.where(yl == 1, got[0][img_half:], got[2][img_half:])
    chunk = jnp.concatenate([mine, other], axis=1)
    mirror = [(a, Z - 1 - a) for a in range(TEXT_Z, Z)]
    chunk = jnp.where(z >= TEXT_Z, chunk, lax.ppermute(chunk, "z", mirror))
    image_all = jnp.concatenate([slabs] + [lax.ppermute(slabs, "x", ring(k)) for k in range(1, 4)])
    chunks = jnp.stack([chunk] + [lax.ppermute(chunk, "z", turn(k)) for k in range(1, TEXT_Z)])
    text_tile = jnp.stack([chunks, swap(chunks, "co")])
    text_tile = text_tile.reshape(2 * TEXT_Z * piece, 2 * width)

    quarter = yl * 2 + yh
    order = jnp.arange(TEXT_Z, dtype=jnp.int32)
    group = jnp.mod(near - order + TEXT_Z, TEXT_Z) * 4 + x
    columns = (
        group[None, :, None] * txt_count
        + jnp.mod(core + jnp.arange(2, dtype=jnp.int32), 2)[:, None, None] * txt_half
        + quarter * piece
        + jnp.arange(piece, dtype=jnp.int32)[None, None, :]
    ).reshape(1, -1)
    padded = jnp.concatenate([pair_perm, jnp.full((16 * img_count,), -1, jnp.int32)])
    padded = pick(pick(padded.reshape(2, Z, 4, 2, img_half), z, 1), core, 2)
    padded = jnp.where(yl == 0, padded, padded[::-1])
    partner = jnp.stack([pick(padded, source, 1) for source in sources]).reshape(-1, 1)
    logit_scale = jnp.exp(log_scale[0])
    weights = [
        jnp.where((side == 1) & (z >= TEXT_Z), 0.0, 1.0).astype(F32) for side in (yl, 1 - yl)
    ]
    factors = jnp.stack([logit_scale, bias[0], *weights])

    image_part, text_part, part_sums = tile_grads(factors, partner, columns, image_all, text_tile)

    text_part = text_part.reshape(2, TEXT_Z, piece, 2 * width)
    both = text_part[0].astype(F32) + swap(text_part[1], "co").astype(F32)
    rounded = both.astype(BF16)
    image_part = image_part.reshape(4, 4, img_half, width)
    text_got = [lax.ppermute(rounded[k], "z", turn(TEXT_Z - k)) for k in range(1, TEXT_Z)]
    image_near = [lax.ppermute(image_part[k], "x", ring(-k)) for k in (1, 3)]
    text_got[:2], image_near, image_far = lax.optimization_barrier(
        (text_got[:2], image_near, image_part[2])
    )
    image_far = lax.ppermute(image_far, "x", ring(-2))
    text_got, image_near, image_far = lax.optimization_barrier((text_got, image_near, image_far))
    text_sum = both[0]
    for g in text_got:
        text_sum = text_sum + g.astype(F32)
    text_round = text_sum.astype(BF16)
    image_sum = image_part[0].astype(F32)
    for g in (*image_near, image_far):
        image_sum = image_sum + g.astype(F32)

    text_round, image_round = lax.optimization_barrier((text_round, image_sum.astype(BF16)))
    image_sum = image_sum[0]
    for k in range(1, 4):
        image_sum = image_sum + y_move(image_round[k], k).astype(F32)
    text_mirror = lax.ppermute(text_round, "z", [(b, a) for a, b in mirror])
    text_sum, text_mirror, image_sum = lax.optimization_barrier(
        (text_sum, text_mirror, image_sum)
    )
    text_sum = (text_sum + text_mirror.astype(F32)).astype(BF16)
    same, cross = text_sum[:, :width], text_sum[:, width:]
    across, straight, diagonal = [y_move(cross if k & 1 else same, k) for k in range(1, 4)]
    cols = width // 2

    def join_cores(rows):
        kept = lax.dynamic_slice_in_dim(rows, core * cols, cols, 1)
        taken = swap(lax.dynamic_slice_in_dim(rows, (1 - core) * cols, cols, 1), "co")
        return jnp.where(
            core == 0,
            jnp.concatenate([kept, taken], axis=0),
            jnp.concatenate([taken, kept], axis=0),
        )

    image_rows = image_sum / lax.dynamic_slice_in_dim(image_norm, core * img_half, img_half, 0)
    image_du = join_cores(image_rows.astype(BF16))
    straight, image_du = lax.optimization_barrier((straight, image_du))
    du_x = [image_du] + [lax.ppermute(image_du, "x", ring(k)) for k in range(1, 4)]
    transposed = (((0,), (0,)), ((), ()))

    text_rows = jnp.where(
        yh == 0,
        jnp.concatenate([straight, diagonal, same, across], axis=0),
        jnp.concatenate([diagonal, straight, across, same], axis=0),
    )
    text_rows = text_rows.astype(F32) / lax.dynamic_slice_in_dim(
        text_norm, core * txt_half, txt_half, 0
    )
    text_du = join_cores(jnp.where(is_text, text_rows, 0.0).astype(BF16))
    text_weight = lax.dot_general(text_hidden, text_du, transposed, preferred_element_type=F32)
    text_share = text_weight.shape[0] // 4
    text_whole = text_weight
    text_weight = text_weight.reshape(4, text_share, cols)
    got = [
        lax.ppermute(pick(text_weight, targets[k]).astype(BF16), "x", ring(k)) for k in range(1, 4)
    ]
    got[0], du_x = lax.optimization_barrier((got[0], du_x))
    image_weight = lax.dot_general(
        jnp.concatenate(hidden_x), jnp.concatenate(du_x), transposed, preferred_element_type=F32
    )
    img_share, txt_share = share_cols // 16, text_share // 16
    own_weight = lax.dynamic_slice_in_dim(img_weight, x * share_cols, share_cols, 0)
    own_gain = lax.dynamic_slice_in_dim(img_gain, x * share_cols, share_cols, 0)
    small = jnp.concatenate(
        [
            jnp.sum(image_weight * own_weight.astype(F32), axis=1) / own_gain,
            jnp.sum(text_whole * txt_weight.astype(F32), axis=1) / txt_gain,
            part_sums[:3, 0],
        ]
    )
    small = small + swap(small, "co")
    small = small + swap(small, "yh")
    text_weight = pick(text_weight, x)
    for g in got:
        text_weight = text_weight + g.astype(F32)

    slot = 32
    spare = slot - img_share
    used = img_share + 4 * txt_share

    def spare_rows(values):
        rows = jnp.stack(split3(values), axis=1)
        return jnp.pad(rows, ((0, 0), (0, spare - 3), (0, cols - values.shape[1])))

    def joined(blocks):
        rows = blocks[..., img_share:slot, :].astype(F32)
        return rows[..., 0, :] + rows[..., 1, :] + rows[..., 2, :]

    sums = jnp.broadcast_to(small[None, share_cols + 4 * text_share :], (16, 3))
    vector = jnp.concatenate(
        [
            small[:share_cols].reshape(16, img_share),
            small[share_cols : share_cols + 4 * text_share].reshape(16, 4 * txt_share),
            sums,
        ],
        axis=1,
    )
    block = jnp.concatenate(
        [
            image_weight.astype(BF16).reshape(16, img_share, cols),
            spare_rows(vector),
            text_weight.astype(BF16).reshape(16, txt_share, cols),
        ],
        axis=1,
    )
    reduced = exchange(block, ("yl", "z"))
    vector = jnp.sum(joined(reduced), axis=0)
    reduced = jnp.sum(reduced.astype(F32), axis=0)
    ready = jnp.concatenate(
        [
            reduced[:img_share].astype(BF16),
            spare_rows(vector[None, : used + 3])[0],
            reduced[slot:].astype(BF16),
        ],
        axis=0,
    )
    gathered = exchange(jnp.broadcast_to(ready, (16, *ready.shape)), ("yl", "z"))
    pieces = [gathered] + [lax.ppermute(gathered, "x", ring(k)) for k in range(1, 4)]
    image_grad, text_grad, vectors = finish(
        jnp.stack(sources), pieces, img_weight.shape[0], txt_weight.shape[0]
    )
    total = jnp.sum(vectors[:, :, img_share : used + 3], axis=0)
    loss_parts = total[0, 4 * txt_share :]
    return (
        loss_parts[0:1] / pair_count,
        image_grad,
        text_grad,
        vectors[:, :, :img_share].reshape(-1),
        total[:, : 4 * txt_share].reshape(-1),
        loss_parts[1:2] * logit_scale,
        loss_parts[2:3],
    )


def solution(mesh):
    inner = Mesh(mesh.devices.reshape(2, Z, 4, 2, 2), ("yl", "z", "x", "yh", "co"))
    tensor = ("yh", "co")
    return jax.shard_map(
        local,
        mesh=inner,
        in_specs=(
            P(DP, None),
            P(DP, None),
            P(),
            P(),
            P(None, tensor),
            P(None, tensor),
            P(),
            P(),
            P(),
        ),
        out_specs=(P(), P(None, tensor), P(None, tensor), P(), P(), P(), P()),
        check_vma=False,
    )
```

```python
import jax
import jax.numpy as jnp
from jax import lax
from jax.experimental import pallas as pl
from jax.experimental.pallas import tpu as pltpu
from jax.sharding import Mesh, PartitionSpec as P

EPS = 1e-06
F32 = jnp.float32
BF16 = jnp.bfloat16
Z = 8
TEXT_Z = 4
DP = ("yl", "z", "x")


def hidden_rows(features, gain_vec):
    values = features.astype(F32)
    center = jnp.mean(values, axis=1, keepdims=True)
    spread = jnp.mean(values * values, axis=1, keepdims=True) - center * center
    scaled = (values - center) * lax.rsqrt(spread + EPS)
    return (scaled * gain_vec).astype(BF16)


def swap(value, axis):
    return lax.ppermute(value, axis, [(0, 1), (1, 0)])


def exchange(value, axes):
    return lax.all_to_all(value, axes, split_axis=0, concat_axis=0, tiled=True)


def split3(value):
    high = value.astype(BF16)
    rest = value - high.astype(F32)
    middle = rest.astype(BF16)
    return high, middle, (rest - middle.astype(F32)).astype(BF16)


def tile_rows(emb_i, i):
    base = 4 * i
    return jnp.concatenate(
        [
            jnp.concatenate([emb_i[base], emb_i[base + 1]], axis=1),
            jnp.concatenate([emb_i[base + 2], emb_i[base + 3]], axis=1),
        ],
        axis=0,
    )


def tile_kernel(
    factors, partner, columns, emb_i, emb_t, out_i, out_t, out_s, acc, sums
):
    scale, shift = factors[0], factors[1]
    high, half = emb_i.shape[1], emb_i.shape[2]
    place = lax.broadcasted_iota(jnp.int32, (2 * high, 1), 0)
    weight = jnp.where(place < high, factors[2], factors[3])
    nt = (((1,), (1,)), ((), ()))
    tn = (((0,), (0,)), ((), ()))

    def grads(similar, i):
        logits = scale * similar + shift
        pair = partner[2 * high * i : 2 * high * (i + 1)] == columns[...]
        signed = jnp.where(pair, -logits, logits)
        small = jnp.exp(-jnp.abs(signed))
        total = 1.0 + small
        inverse = 1.0 / total
        sigmoid = jnp.where(signed >= 0, inverse, small * inverse)
        soft = jnp.maximum(signed, 0.0) + jnp.log(total) + (small - (total - 1.0)) * inverse
        grad = jnp.where(pair, -sigmoid, sigmoid) * weight
        parts = [
            jnp.sum(soft * weight, axis=0, keepdims=True),
            jnp.sum(grad * similar, axis=0, keepdims=True),
            jnp.sum(grad, axis=0, keepdims=True),
        ]
        for j, part in enumerate(parts):
            if i == 0:
                sums[j : j + 1] = part
            else:
                sums[j : j + 1] += part
        return grad.astype(BF16)

    def finish_rows(rounded, rows, i):
        update = lax.dot_general(rounded, rows, tn, preferred_element_type=F32)
        if i == 0:
            acc[...] = update
        else:
            acc[...] += update
        grad_rows = jnp.dot(rounded, emb_t[...], preferred_element_type=F32)
        wide = rows.astype(F32)
        inner = jnp.sum(wide * grad_rows, axis=1, keepdims=True)
        result = (scale * (grad_rows - wide * inner)).astype(BF16)
        out_i[4 * i] = result[:high, :half]
        out_i[4 * i + 1] = result[:high, half:]
        out_i[4 * i + 2] = result[high:, :half]
        out_i[4 * i + 3] = result[high:, half:]

    rows = tile_rows(emb_i, 0)
    similar = lax.dot_general(rows, emb_t[...], nt, preferred_element_type=F32)
    for i in range(4):
        if i < 3:
            later = tile_rows(emb_i, i + 1)
            ahead = lax.dot_general(later, emb_t[...], nt, preferred_element_type=F32)
        rounded = grads(similar, i)
        finish_rows(rounded, rows, i)
        if i < 3:
            rows, similar = later, ahead
    sums[3:] = jnp.zeros_like(sums[3:])
    texts = emb_t[...].astype(F32)
    grads_t = acc[...]
    inner = jnp.sum(texts * grads_t, axis=1, keepdims=True)
    out_t[...] = (scale * (grads_t - texts * inner)).astype(BF16)
    out_s[...] = jnp.broadcast_to(jnp.sum(sums[...], axis=1, keepdims=True), out_s.shape)


def tile_grads(factors, partner, columns, emb_i, emb_t):
    count, width = emb_t.shape
    whole = pl.BlockSpec(memory_space=pltpu.VMEM)
    return pl.pallas_call(
        tile_kernel,
        in_specs=[pl.BlockSpec(memory_space=pltpu.SMEM)] + [whole] * 4,
        out_specs=[whole] * 3,
        out_shape=[
            jax.ShapeDtypeStruct(emb_i.shape, BF16),
            jax.ShapeDtypeStruct(emb_t.shape, BF16),
            jax.ShapeDtypeStruct((8, 128), F32),
        ],
        scratch_shapes=[pltpu.VMEM((count, width), F32), pltpu.VMEM((8, count), F32)],
        compiler_params=pltpu.CompilerParams(vmem_limit_bytes=40 * 1024 * 1024),
    )(factors, partner, columns, emb_i, emb_t)


def half_place(half, j):
    return TEXT_Z + j if half else TEXT_Z - 1 - j


def turn(k):
    return [
        (half_place(half, j), half_place(half, (j + k) % TEXT_Z))
        for half in range(2)
        for j in range(TEXT_Z)
    ]


def finish_kernel(places, first, second, third, fourth, out_i, out_t, out_g, rows):
    image_rows = rows.shape[0] // 16
    text_rows = out_t.shape[0] // 64
    padded = first.shape[1] - text_rows
    for k, piece in enumerate((first, second, third, fourth)):
        place = places[k]
        for s in range(16):
            values = piece[s].astype(F32)
            rows[s * image_rows : (s + 1) * image_rows] = values[:image_rows]
            start = pl.multiple_of(place * (16 * text_rows) + s * text_rows, 8)
            out_t[pl.ds(start, text_rows)] = values[padded:]
            tail = values[image_rows:padded]
            out_g[place, s : s + 1] = tail[0:1] + tail[1:2] + tail[2:3]
        start = pl.multiple_of(place * (16 * image_rows), 8)
        out_i[pl.ds(start, 16 * image_rows)] = rows[...]


def finish(places, pieces, image_total, text_total):
    cols = pieces[0].shape[2]
    whole = pl.BlockSpec(memory_space=pltpu.VMEM)
    return pl.pallas_call(
        finish_kernel,
        in_specs=[pl.BlockSpec(memory_space=pltpu.SMEM)] + [whole] * 4,
        out_specs=[whole] * 3,
        out_shape=[
            jax.ShapeDtypeStruct((image_total, cols), F32),
            jax.ShapeDtypeStruct((text_total, cols), F32),
            jax.ShapeDtypeStruct((4, 16, cols), F32),
        ],
        scratch_shapes=[pltpu.VMEM((image_total // 4, cols), F32)],
        compiler_params=pltpu.CompilerParams(vmem_limit_bytes=24 * 1024 * 1024),
    )(places, *pieces)


def ring(k):
    return [(i, (i + k) % 4) for i in range(4)]


def y_move(value, k):
    return lax.ppermute(value, ("yl", "yh"), [(i, i ^ k) for i in range(4)])


def pick(value, index, axis=0):
    return lax.dynamic_index_in_dim(value, index, axis, keepdims=False)


def local(
    img_feats, txt_feats, img_gain, txt_gain, img_weight, txt_weight, log_scale, bias, pair_perm
):
    yl, z, x = lax.axis_index("yl"), lax.axis_index("z"), lax.axis_index("x")
    yh, core = lax.axis_index("yh"), lax.axis_index("co")
    pair_count = pair_perm.shape[0]
    img_count, txt_count = img_feats.shape[0], txt_feats.shape[0]
    img_half, txt_half = img_count // 2, txt_count // 2
    piece = txt_half // 4
    is_text = (yl == 1) & (z >= TEXT_Z)
    near = jnp.where(z >= TEXT_Z, z - TEXT_Z, TEXT_Z - 1 - z)
    sources = [jnp.mod(x - k + 4, 4) for k in range(4)]
    targets = [jnp.mod(x + k, 4) for k in range(4)]

    image_hidden = hidden_rows(img_feats, img_gain)
    image_hidden, text_gain = lax.optimization_barrier((image_hidden, txt_gain))
    text_hidden = hidden_rows(txt_feats, text_gain)
    share_cols = image_hidden.shape[1] // 4
    parts = jnp.stack(
        [image_hidden[:, i * share_cols : (i + 1) * share_cols] for i in range(4)]
    )
    hidden_x = [pick(parts, x)]
    hidden_x += [lax.ppermute(pick(parts, targets[k]), "x", ring(k)) for k in range(1, 4)]

    text_proj = jnp.dot(text_hidden, txt_weight, preferred_element_type=F32)
    image_proj = jnp.dot(image_hidden, img_weight, preferred_element_type=F32)
    squares = jnp.concatenate(
        [jnp.sum(text_proj * text_proj, axis=1), jnp.sum(image_proj * image_proj, axis=1)]
    )
    squares = squares + swap(squares, "co")
    squares = squares + swap(squares, "yh")
    norms = jnp.sqrt(squares + EPS)[:, None]
    text_norm, image_norm = norms[:txt_count], norms[txt_count:]
    text_emb = (text_proj / text_norm).astype(BF16)
    image_emb = (image_proj / image_norm).astype(BF16)

    def halves(index):
        return jnp.concatenate(
            [
                lax.dynamic_slice_in_dim(image_emb, index * img_half, img_half, 0),
                lax.dynamic_slice_in_dim(text_emb, index * txt_half, txt_half, 0),
            ],
            axis=0,
        )

    kept = halves(core)
    taken = swap(halves(1 - core), "co")
    both = jnp.where(
        core == 0,
        jnp.concatenate([kept, taken], axis=1),
        jnp.concatenate([taken, kept], axis=1),
    )
    width = both.shape[1]
    image_own = both[:img_half]
    text_own = both[img_half:].reshape(4, piece, width)

    got = []
    for k in range(1, 4):
        target = jnp.bitwise_xor(yl * 2 + yh, k)
        got.append(y_move(jnp.concatenate([image_own, pick(text_own, target)], axis=0), k))
    got, hidden_x = lax.optimization_barrier((got, hidden_x))
    slabs = jnp.stack([image_own] + [g[:img_half] for g in got])
    mine = jnp.where(yl == 1, pick(text_own, yl * 2 + yh), got[1][img_half:])
    other = jnp.where(yl == 1, got[0][img_half:], got[2][img_half:])
    chunk = jnp.concatenate([mine, other], axis=1)
    mirror = [(a, Z - 1 - a) for a in range(TEXT_Z, Z)]
    chunk = jnp.where(z >= TEXT_Z, chunk, lax.ppermute(chunk, "z", mirror))
    image_all = jnp.concatenate([slabs] + [lax.ppermute(slabs, "x", ring(k)) for k in range(1, 4)])
    chunks = [chunk] + [lax.ppermute(chunk, "z", turn(k)) for k in (1, 2)]
    chunks[1], last = lax.optimization_barrier((chunks[1], chunk))
    chunks = jnp.stack([*chunks, lax.ppermute(last, "z", turn(3))])
    text_tile = jnp.stack([chunks, swap(chunks, "co")])
    text_tile = text_tile.reshape(2 * TEXT_Z * piece, 2 * width)

    quarter = yl * 2 + yh
    order = jnp.arange(TEXT_Z, dtype=jnp.int32)
    group = jnp.mod(near - order + TEXT_Z, TEXT_Z) * 4 + x
    columns = (
        group[None, :, None] * txt_count
        + jnp.mod(core + jnp.arange(2, dtype=jnp.int32), 2)[:, None, None] * txt_half
        + quarter * piece
        + jnp.arange(piece, dtype=jnp.int32)[None, None, :]
    ).reshape(1, -1)
    padded = jnp.concatenate([pair_perm, jnp.full((16 * img_count,), -1, jnp.int32)])
    padded = pick(pick(padded.reshape(2, Z, 4, 2, img_half), z, 1), core, 2)
    padded = jnp.where(yl == 0, padded, padded[::-1])
    partner = jnp.stack([pick(padded, source, 1) for source in sources]).reshape(-1, 1)
    logit_scale = jnp.exp(log_scale[0])
    weights = [
        jnp.where((side == 1) & (z >= TEXT_Z), 0.0, 1.0).astype(F32) for side in (yl, 1 - yl)
    ]
    factors = jnp.stack([logit_scale, bias[0], *weights])

    image_part, text_part, part_sums = tile_grads(factors, partner, columns, image_all, text_tile)

    text_part = text_part.reshape(2, TEXT_Z, piece, 2 * width)
    both = text_part[0].astype(F32) + swap(text_part[1], "co").astype(F32)
    rounded = both.astype(BF16)
    image_part = image_part.reshape(4, 4, img_half, width)
    text_got = [lax.ppermute(rounded[k], "z", turn(TEXT_Z - k)) for k in (1, 2)]
    text_got[0], last = lax.optimization_barrier((text_got[0], rounded[3]))
    text_got.append(lax.ppermute(last, "z", turn(1)))
    image_near = [lax.ppermute(image_part[k], "x", ring(-k)) for k in (1, 3)]
    image_far = lax.ppermute(image_part[2], "x", ring(-2))
    text_got, image_near, image_far = lax.optimization_barrier((text_got, image_near, image_far))
    text_sum = both[0]
    for g in text_got:
        text_sum = text_sum + g.astype(F32)
    text_round = text_sum.astype(BF16)
    image_sum = image_part[0].astype(F32)
    for g in (*image_near, image_far):
        image_sum = image_sum + g.astype(F32)

    text_round, image_round = lax.optimization_barrier((text_round, image_sum.astype(BF16)))
    image_sum = image_sum[0]
    for k in range(1, 4):
        image_sum = image_sum + y_move(image_round[k], k).astype(F32)
    text_mirror = lax.ppermute(text_round, "z", [(b, a) for a, b in mirror])
    text_sum, text_mirror, image_sum = lax.optimization_barrier(
        (text_sum, text_mirror, image_sum)
    )
    text_sum = (text_sum + text_mirror.astype(F32)).astype(BF16)
    same, cross = text_sum[:, :width], text_sum[:, width:]
    across, straight, diagonal = [y_move(cross if k & 1 else same, k) for k in range(1, 4)]
    cols = width // 2

    def join_cores(rows):
        kept = lax.dynamic_slice_in_dim(rows, core * cols, cols, 1)
        taken = swap(lax.dynamic_slice_in_dim(rows, (1 - core) * cols, cols, 1), "co")
        return jnp.where(
            core == 0,
            jnp.concatenate([kept, taken], axis=0),
            jnp.concatenate([taken, kept], axis=0),
        )

    image_rows = image_sum / lax.dynamic_slice_in_dim(image_norm, core * img_half, img_half, 0)
    image_du = join_cores(image_rows.astype(BF16))
    straight, image_du = lax.optimization_barrier((straight, image_du))
    du_x = [image_du] + [lax.ppermute(image_du, "x", ring(k)) for k in range(1, 4)]
    transposed = (((0,), (0,)), ((), ()))

    text_rows = jnp.where(
        yh == 0,
        jnp.concatenate([straight, diagonal, same, across], axis=0),
        jnp.concatenate([diagonal, straight, across, same], axis=0),
    )
    text_rows = text_rows.astype(F32) / lax.dynamic_slice_in_dim(
        text_norm, core * txt_half, txt_half, 0
    )
    text_du = join_cores(jnp.where(is_text, text_rows, 0.0).astype(BF16))
    text_weight = lax.dot_general(text_hidden, text_du, transposed, preferred_element_type=F32)
    text_share = text_weight.shape[0] // 4
    text_whole = text_weight
    text_weight = text_weight.reshape(4, text_share, cols)
    got = [
        lax.ppermute(pick(text_weight, targets[k]).astype(BF16), "x", ring(k)) for k in range(1, 4)
    ]
    got[0], du_x = lax.optimization_barrier((got[0], du_x))
    image_weight = lax.dot_general(
        jnp.concatenate(hidden_x), jnp.concatenate(du_x), transposed, preferred_element_type=F32
    )
    img_share, txt_share = share_cols // 16, text_share // 16
    own_weight = lax.dynamic_slice_in_dim(img_weight, x * share_cols, share_cols, 0)
    own_gain = lax.dynamic_slice_in_dim(img_gain, x * share_cols, share_cols, 0)
    small = jnp.concatenate(
        [
            jnp.sum(image_weight * own_weight.astype(F32), axis=1) / own_gain,
            jnp.sum(text_whole * txt_weight.astype(F32), axis=1) / txt_gain,
            part_sums[:3, 0],
        ]
    )
    small = small + swap(small, "co")
    small = small + swap(small, "yh")
    text_weight = pick(text_weight, x)
    for g in got:
        text_weight = text_weight + g.astype(F32)

    slot = 32
    spare = slot - img_share
    used = img_share + 4 * txt_share

    def spare_rows(values):
        rows = jnp.stack(split3(values), axis=1)
        return jnp.pad(rows, ((0, 0), (0, spare - 3), (0, cols - values.shape[1])))

    def joined(blocks):
        rows = blocks[..., img_share:slot, :].astype(F32)
        return rows[..., 0, :] + rows[..., 1, :] + rows[..., 2, :]

    sums = jnp.broadcast_to(small[None, share_cols + 4 * text_share :], (16, 3))
    vector = jnp.concatenate(
        [
            small[:share_cols].reshape(16, img_share),
            small[share_cols : share_cols + 4 * text_share].reshape(16, 4 * txt_share),
            sums,
        ],
        axis=1,
    )
    block = jnp.concatenate(
        [
            image_weight.astype(BF16).reshape(16, img_share, cols),
            spare_rows(vector),
            text_weight.astype(BF16).reshape(16, txt_share, cols),
        ],
        axis=1,
    )
    reduced = exchange(block, ("yl", "z"))
    vector = jnp.sum(joined(reduced), axis=0)
    reduced = jnp.sum(reduced.astype(F32), axis=0)
    ready = jnp.concatenate(
        [
            reduced[:img_share].astype(BF16),
            spare_rows(vector[None, : used + 3])[0],
            reduced[slot:].astype(BF16),
        ],
        axis=0,
    )
    gathered = exchange(jnp.broadcast_to(ready, (16, *ready.shape)), ("yl", "z"))
    pieces = [gathered] + [lax.ppermute(gathered, "x", ring(k)) for k in range(1, 4)]
    image_grad, text_grad, vectors = finish(
        jnp.stack(sources), pieces, img_weight.shape[0], txt_weight.shape[0]
    )
    total = jnp.sum(vectors[:, :, img_share : used + 3], axis=0)
    loss_parts = total[0, 4 * txt_share :]
    return (
        loss_parts[0:1] / pair_count,
        image_grad,
        text_grad,
        vectors[:, :, :img_share].reshape(-1),
        total[:, : 4 * txt_share].reshape(-1),
        loss_parts[1:2] * logit_scale,
        loss_parts[2:3],
    )


def solution(mesh):
    inner = Mesh(mesh.devices.reshape(2, Z, 4, 2, 2), ("yl", "z", "x", "yh", "co"))
    tensor = ("yh", "co")
    return jax.shard_map(
        local,
        mesh=inner,
        in_specs=(
            P(DP, None),
            P(DP, None),
            P(),
            P(),
            P(None, tensor),
            P(None, tensor),
            P(),
            P(),
            P(),
        ),
        out_specs=(P(), P(None, tensor), P(None, tensor), P(), P(), P(), P()),
        check_vma=False,
    )
```

```python
import jax
import jax.numpy as jnp
from jax import lax
from jax.experimental import pallas as pl
from jax.experimental.pallas import tpu as pltpu
from jax.sharding import Mesh, PartitionSpec as P

EPS = 1e-06
F32 = jnp.float32
BF16 = jnp.bfloat16
Z = 8
TEXT_Z = 4
DP = ("yl", "z", "x")


def hidden_rows(features, gain_vec):
    values = features.astype(F32)
    center = jnp.mean(values, axis=1, keepdims=True)
    spread = jnp.mean(values * values, axis=1, keepdims=True) - center * center
    scaled = (values - center) * lax.rsqrt(spread + EPS)
    return (scaled * gain_vec).astype(BF16)


def swap(value, axis):
    return lax.ppermute(value, axis, [(0, 1), (1, 0)])


def exchange(value, axes):
    return lax.all_to_all(value, axes, split_axis=0, concat_axis=0, tiled=True)


def split3(value):
    high = value.astype(BF16)
    rest = value - high.astype(F32)
    middle = rest.astype(BF16)
    return high, middle, (rest - middle.astype(F32)).astype(BF16)


def tile_rows(emb_i, i):
    base = 4 * i
    return jnp.concatenate(
        [
            jnp.concatenate([emb_i[base], emb_i[base + 1]], axis=1),
            jnp.concatenate([emb_i[base + 2], emb_i[base + 3]], axis=1),
        ],
        axis=0,
    )


def tile_kernel(
    factors, partner, columns, emb_i, emb_t, out_i, out_t, out_s, acc, sums
):
    scale, shift = factors[0], factors[1]
    high, half = emb_i.shape[1], emb_i.shape[2]
    place = lax.broadcasted_iota(jnp.int32, (2 * high, 1), 0)
    weight = jnp.where(place < high, factors[2], factors[3])
    nt = (((1,), (1,)), ((), ()))
    tn = (((0,), (0,)), ((), ()))

    def grads(similar, i):
        logits = scale * similar + shift
        pair = partner[2 * high * i : 2 * high * (i + 1)] == columns[...]
        signed = jnp.where(pair, -logits, logits)
        small = jnp.exp(-jnp.abs(signed))
        total = 1.0 + small
        inverse = 1.0 / total
        sigmoid = jnp.where(signed >= 0, inverse, small * inverse)
        soft = jnp.maximum(signed, 0.0) + jnp.log(total) + (small - (total - 1.0)) * inverse
        grad = jnp.where(pair, -sigmoid, sigmoid) * weight
        parts = [
            jnp.sum(soft * weight, axis=0, keepdims=True),
            jnp.sum(grad * similar, axis=0, keepdims=True),
            jnp.sum(grad, axis=0, keepdims=True),
        ]
        for j, part in enumerate(parts):
            if i == 0:
                sums[j : j + 1] = part
            else:
                sums[j : j + 1] += part
        return grad.astype(BF16)

    def finish_rows(rounded, rows, i):
        update = lax.dot_general(rounded, rows, tn, preferred_element_type=F32)
        if i == 0:
            acc[...] = update
        else:
            acc[...] += update
        grad_rows = jnp.dot(rounded, emb_t[...], preferred_element_type=F32)
        wide = rows.astype(F32)
        inner = jnp.sum(wide * grad_rows, axis=1, keepdims=True)
        result = (scale * (grad_rows - wide * inner)).astype(BF16)
        out_i[4 * i] = result[:high, :half]
        out_i[4 * i + 1] = result[:high, half:]
        out_i[4 * i + 2] = result[high:, :half]
        out_i[4 * i + 3] = result[high:, half:]

    rows = tile_rows(emb_i, 0)
    similar = lax.dot_general(rows, emb_t[...], nt, preferred_element_type=F32)
    for i in range(4):
        if i < 3:
            later = tile_rows(emb_i, i + 1)
            ahead = lax.dot_general(later, emb_t[...], nt, preferred_element_type=F32)
        rounded = grads(similar, i)
        finish_rows(rounded, rows, i)
        if i < 3:
            rows, similar = later, ahead
    sums[3:] = jnp.zeros_like(sums[3:])
    texts = emb_t[...].astype(F32)
    grads_t = acc[...]
    inner = jnp.sum(texts * grads_t, axis=1, keepdims=True)
    out_t[...] = (scale * (grads_t - texts * inner)).astype(BF16)
    out_s[...] = jnp.broadcast_to(jnp.sum(sums[...], axis=1, keepdims=True), out_s.shape)


def tile_grads(factors, partner, columns, emb_i, emb_t):
    count, width = emb_t.shape
    whole = pl.BlockSpec(memory_space=pltpu.VMEM)
    return pl.pallas_call(
        tile_kernel,
        in_specs=[pl.BlockSpec(memory_space=pltpu.SMEM)] + [whole] * 4,
        out_specs=[whole] * 3,
        out_shape=[
            jax.ShapeDtypeStruct(emb_i.shape, BF16),
            jax.ShapeDtypeStruct(emb_t.shape, BF16),
            jax.ShapeDtypeStruct((8, 128), F32),
        ],
        scratch_shapes=[pltpu.VMEM((count, width), F32), pltpu.VMEM((8, count), F32)],
        compiler_params=pltpu.CompilerParams(vmem_limit_bytes=40 * 1024 * 1024),
    )(factors, partner, columns, emb_i, emb_t)


def half_place(half, j):
    return TEXT_Z + j if half else TEXT_Z - 1 - j


def turn(k):
    return [
        (half_place(half, j), half_place(half, (j + k) % TEXT_Z))
        for half in range(2)
        for j in range(TEXT_Z)
    ]


def finish_kernel(places, first, second, third, fourth, out_i, out_t, out_g, rows):
    image_rows = rows.shape[0] // 16
    text_rows = out_t.shape[0] // 64
    padded = first.shape[1] - text_rows
    for k, piece in enumerate((first, second, third, fourth)):
        place = places[k]
        for s in range(16):
            values = piece[s].astype(F32)
            rows[s * image_rows : (s + 1) * image_rows] = values[:image_rows]
            start = pl.multiple_of(place * (16 * text_rows) + s * text_rows, 8)
            out_t[pl.ds(start, text_rows)] = values[padded:]
            tail = values[image_rows:padded]
            out_g[place, s : s + 1] = tail[0:1] + tail[1:2] + tail[2:3]
        start = pl.multiple_of(place * (16 * image_rows), 8)
        out_i[pl.ds(start, 16 * image_rows)] = rows[...]


def finish(places, pieces, image_total, text_total):
    cols = pieces[0].shape[2]
    whole = pl.BlockSpec(memory_space=pltpu.VMEM)
    return pl.pallas_call(
        finish_kernel,
        in_specs=[pl.BlockSpec(memory_space=pltpu.SMEM)] + [whole] * 4,
        out_specs=[whole] * 3,
        out_shape=[
            jax.ShapeDtypeStruct((image_total, cols), F32),
            jax.ShapeDtypeStruct((text_total, cols), F32),
            jax.ShapeDtypeStruct((4, 16, cols), F32),
        ],
        scratch_shapes=[pltpu.VMEM((image_total // 4, cols), F32)],
        compiler_params=pltpu.CompilerParams(vmem_limit_bytes=24 * 1024 * 1024),
    )(places, *pieces)


def ring(k):
    return [(i, (i + k) % 4) for i in range(4)]


def y_move(value, k):
    return lax.ppermute(value, ("yl", "yh"), [(i, i ^ k) for i in range(4)])


def pick(value, index, axis=0):
    return lax.dynamic_index_in_dim(value, index, axis, keepdims=False)


def local(
    img_feats, txt_feats, img_gain, txt_gain, img_weight, txt_weight, log_scale, bias, pair_perm
):
    yl, z, x = lax.axis_index("yl"), lax.axis_index("z"), lax.axis_index("x")
    yh, core = lax.axis_index("yh"), lax.axis_index("co")
    pair_count = pair_perm.shape[0]
    img_count, txt_count = img_feats.shape[0], txt_feats.shape[0]
    img_half, txt_half = img_count // 2, txt_count // 2
    piece = txt_half // 4
    is_text = (yl == 1) & (z >= TEXT_Z)
    near = jnp.where(z >= TEXT_Z, z - TEXT_Z, TEXT_Z - 1 - z)
    sources = [jnp.mod(x - k + 4, 4) for k in range(4)]
    targets = [jnp.mod(x + k, 4) for k in range(4)]

    image_hidden = hidden_rows(img_feats, img_gain)
    image_hidden, text_gain = lax.optimization_barrier((image_hidden, txt_gain))
    text_hidden = hidden_rows(txt_feats, text_gain)
    share_cols = image_hidden.shape[1] // 4
    parts = jnp.stack(
        [image_hidden[:, i * share_cols : (i + 1) * share_cols] for i in range(4)]
    )
    hidden_x = [pick(parts, x)]
    hidden_x += [lax.ppermute(pick(parts, targets[k]), "x", ring(k)) for k in range(1, 4)]

    text_proj = jnp.dot(text_hidden, txt_weight, preferred_element_type=F32)
    image_proj = jnp.dot(image_hidden, img_weight, preferred_element_type=F32)
    squares = jnp.concatenate(
        [jnp.sum(text_proj * text_proj, axis=1), jnp.sum(image_proj * image_proj, axis=1)]
    )
    squares = squares + swap(squares, "co")
    squares = squares + swap(squares, "yh")
    norms = jnp.sqrt(squares + EPS)[:, None]
    text_norm, image_norm = norms[:txt_count], norms[txt_count:]
    text_emb = (text_proj / text_norm).astype(BF16)
    image_emb = (image_proj / image_norm).astype(BF16)

    def halves(index):
        return jnp.concatenate(
            [
                lax.dynamic_slice_in_dim(image_emb, index * img_half, img_half, 0),
                lax.dynamic_slice_in_dim(text_emb, index * txt_half, txt_half, 0),
            ],
            axis=0,
        )

    kept = halves(core)
    taken = swap(halves(1 - core), "co")
    both = jnp.where(
        core == 0,
        jnp.concatenate([kept, taken], axis=1),
        jnp.concatenate([taken, kept], axis=1),
    )
    width = both.shape[1]
    image_own = both[:img_half]
    text_own = both[img_half:].reshape(4, piece, width)

    got = []
    for k in range(1, 4):
        target = jnp.bitwise_xor(yl * 2 + yh, k)
        got.append(y_move(jnp.concatenate([image_own, pick(text_own, target)], axis=0), k))
    got, hidden_x = lax.optimization_barrier((got, hidden_x))
    slabs = jnp.stack([image_own] + [g[:img_half] for g in got])
    mine = jnp.where(yl == 1, pick(text_own, yl * 2 + yh), got[1][img_half:])
    other = jnp.where(yl == 1, got[0][img_half:], got[2][img_half:])
    chunk = jnp.concatenate([mine, other], axis=1)
    mirror = [(a, Z - 1 - a) for a in range(TEXT_Z, Z)]
    chunk = jnp.where(z >= TEXT_Z, chunk, lax.ppermute(chunk, "z", mirror))
    image_all = jnp.concatenate([slabs] + [lax.ppermute(slabs, "x", ring(k)) for k in range(1, 4)])
    chunks = jnp.stack([chunk] + [lax.ppermute(chunk, "z", turn(k)) for k in range(1, TEXT_Z)])
    text_tile = jnp.stack([chunks, swap(chunks, "co")])
    text_tile = text_tile.reshape(2 * TEXT_Z * piece, 2 * width)

    quarter = yl * 2 + yh
    order = jnp.arange(TEXT_Z, dtype=jnp.int32)
    group = jnp.mod(near - order + TEXT_Z, TEXT_Z) * 4 + x
    columns = (
        group[None, :, None] * txt_count
        + jnp.mod(core + jnp.arange(2, dtype=jnp.int32), 2)[:, None, None] * txt_half
        + quarter * piece
        + jnp.arange(piece, dtype=jnp.int32)[None, None, :]
    ).reshape(1, -1)
    padded = jnp.concatenate([pair_perm, jnp.full((16 * img_count,), -1, jnp.int32)])
    padded = pick(pick(padded.reshape(2, Z, 4, 2, img_half), z, 1), core, 2)
    padded = jnp.where(yl == 0, padded, padded[::-1])
    partner = jnp.stack([pick(padded, source, 1) for source in sources]).reshape(-1, 1)
    logit_scale = jnp.exp(log_scale[0])
    weights = [
        jnp.where((side == 1) & (z >= TEXT_Z), 0.0, 1.0).astype(F32) for side in (yl, 1 - yl)
    ]
    factors = jnp.stack([logit_scale, bias[0], *weights])

    image_part, text_part, part_sums = tile_grads(factors, partner, columns, image_all, text_tile)

    text_part = text_part.reshape(2, TEXT_Z, piece, 2 * width)
    both = text_part[0].astype(F32) + swap(text_part[1], "co").astype(F32)
    rounded = both.astype(BF16)
    image_part = image_part.reshape(4, 4, img_half, width)
    text_got = [lax.ppermute(rounded[k], "z", turn(TEXT_Z - k)) for k in (1, 2)]
    text_got[0], last = lax.optimization_barrier((text_got[0], rounded[3]))
    text_got.append(lax.ppermute(last, "z", turn(1)))
    image_near = [lax.ppermute(image_part[k], "x", ring(-k)) for k in (1, 3)]
    image_far = lax.ppermute(image_part[2], "x", ring(-2))
    text_got, image_near, image_far = lax.optimization_barrier((text_got, image_near, image_far))
    text_sum = both[0]
    for g in text_got:
        text_sum = text_sum + g.astype(F32)
    text_round = text_sum.astype(BF16)
    image_sum = image_part[0].astype(F32)
    for g in (*image_near, image_far):
        image_sum = image_sum + g.astype(F32)

    text_round, image_round = lax.optimization_barrier((text_round, image_sum.astype(BF16)))
    image_sum = image_sum[0]
    for k in range(1, 4):
        image_sum = image_sum + y_move(image_round[k], k).astype(F32)
    text_mirror = lax.ppermute(text_round, "z", [(b, a) for a, b in mirror])
    text_sum, text_mirror, image_sum = lax.optimization_barrier(
        (text_sum, text_mirror, image_sum)
    )
    text_sum = (text_sum + text_mirror.astype(F32)).astype(BF16)
    same, cross = text_sum[:, :width], text_sum[:, width:]
    across, straight, diagonal = [y_move(cross if k & 1 else same, k) for k in range(1, 4)]
    cols = width // 2

    def join_cores(rows):
        kept = lax.dynamic_slice_in_dim(rows, core * cols, cols, 1)
        taken = swap(lax.dynamic_slice_in_dim(rows, (1 - core) * cols, cols, 1), "co")
        return jnp.where(
            core == 0,
            jnp.concatenate([kept, taken], axis=0),
            jnp.concatenate([taken, kept], axis=0),
        )

    image_rows = image_sum / lax.dynamic_slice_in_dim(image_norm, core * img_half, img_half, 0)
    image_du = join_cores(image_rows.astype(BF16))
    straight, image_du = lax.optimization_barrier((straight, image_du))
    du_x = [image_du] + [lax.ppermute(image_du, "x", ring(k)) for k in range(1, 4)]
    transposed = (((0,), (0,)), ((), ()))

    text_rows = jnp.where(
        yh == 0,
        jnp.concatenate([straight, diagonal, same, across], axis=0),
        jnp.concatenate([diagonal, straight, across, same], axis=0),
    )
    text_rows = text_rows.astype(F32) / lax.dynamic_slice_in_dim(
        text_norm, core * txt_half, txt_half, 0
    )
    text_du = join_cores(jnp.where(is_text, text_rows, 0.0).astype(BF16))
    text_weight = lax.dot_general(text_hidden, text_du, transposed, preferred_element_type=F32)
    text_share = text_weight.shape[0] // 4
    text_whole = text_weight
    text_weight = text_weight.reshape(4, text_share, cols)
    got = [
        lax.ppermute(pick(text_weight, targets[k]).astype(BF16), "x", ring(k)) for k in range(1, 4)
    ]
    got[0], du_x = lax.optimization_barrier((got[0], du_x))
    image_weight = lax.dot_general(
        jnp.concatenate(hidden_x), jnp.concatenate(du_x), transposed, preferred_element_type=F32
    )
    img_share, txt_share = share_cols // 16, text_share // 16
    own_weight = lax.dynamic_slice_in_dim(img_weight, x * share_cols, share_cols, 0)
    own_gain = lax.dynamic_slice_in_dim(img_gain, x * share_cols, share_cols, 0)
    small = jnp.concatenate(
        [
            jnp.sum(image_weight * own_weight.astype(F32), axis=1) / own_gain,
            jnp.sum(text_whole * txt_weight.astype(F32), axis=1) / txt_gain,
            part_sums[:3, 0],
        ]
    )
    small = small + swap(small, "co")
    small = small + swap(small, "yh")
    text_weight = pick(text_weight, x)
    for g in got:
        text_weight = text_weight + g.astype(F32)

    slot = 32
    spare = slot - img_share
    used = img_share + 4 * txt_share

    def spare_rows(values):
        rows = jnp.stack(split3(values), axis=1)
        return jnp.pad(rows, ((0, 0), (0, spare - 3), (0, cols - values.shape[1])))

    def joined(blocks):
        rows = blocks[..., img_share:slot, :].astype(F32)
        return rows[..., 0, :] + rows[..., 1, :] + rows[..., 2, :]

    sums = jnp.broadcast_to(small[None, share_cols + 4 * text_share :], (16, 3))
    vector = jnp.concatenate(
        [
            small[:share_cols].reshape(16, img_share),
            small[share_cols : share_cols + 4 * text_share].reshape(16, 4 * txt_share),
            sums,
        ],
        axis=1,
    )
    block = jnp.concatenate(
        [
            image_weight.astype(BF16).reshape(16, img_share, cols),
            spare_rows(vector),
            text_weight.astype(BF16).reshape(16, txt_share, cols),
        ],
        axis=1,
    )
    reduced = exchange(block, ("yl", "z"))
    vector = jnp.sum(joined(reduced), axis=0)
    reduced = jnp.sum(reduced.astype(F32), axis=0)
    ready = jnp.concatenate(
        [
            reduced[:img_share].astype(BF16),
            spare_rows(vector[None, : used + 3])[0],
            reduced[slot:].astype(BF16),
        ],
        axis=0,
    )
    gathered = exchange(jnp.broadcast_to(ready, (16, *ready.shape)), ("yl", "z"))
    pieces = [gathered] + [lax.ppermute(gathered, "x", ring(k)) for k in range(1, 4)]
    image_grad, text_grad, vectors = finish(
        jnp.stack(sources), pieces, img_weight.shape[0], txt_weight.shape[0]
    )
    total = jnp.sum(vectors[:, :, img_share : used + 3], axis=0)
    loss_parts = total[0, 4 * txt_share :]
    return (
        loss_parts[0:1] / pair_count,
        image_grad,
        text_grad,
        vectors[:, :, :img_share].reshape(-1),
        total[:, : 4 * txt_share].reshape(-1),
        loss_parts[1:2] * logit_scale,
        loss_parts[2:3],
    )


def solution(mesh):
    inner = Mesh(mesh.devices.reshape(2, Z, 4, 2, 2), ("yl", "z", "x", "yh", "co"))
    tensor = ("yh", "co")
    return jax.shard_map(
        local,
        mesh=inner,
        in_specs=(
            P(DP, None),
            P(DP, None),
            P(),
            P(),
            P(None, tensor),
            P(None, tensor),
            P(),
            P(),
            P(),
        ),
        out_specs=(P(), P(None, tensor), P(None, tensor), P(), P(), P(), P()),
        check_vma=False,
    )
```

```python
import jax
import jax.numpy as jnp
from jax import lax
from jax.experimental import pallas as pl
from jax.experimental.pallas import tpu as pltpu
from jax.sharding import Mesh, PartitionSpec as P

EPS = 1e-06
F32 = jnp.float32
BF16 = jnp.bfloat16
Z = 8
TEXT_Z = 4
DP = ("yl", "z", "x")


def hidden_rows(features, gain_vec):
    values = features.astype(F32)
    center = jnp.mean(values, axis=1, keepdims=True)
    spread = jnp.mean(values * values, axis=1, keepdims=True) - center * center
    scaled = (values - center) * lax.rsqrt(spread + EPS)
    return (scaled * gain_vec).astype(BF16)


def swap(value, axis):
    return lax.ppermute(value, axis, [(0, 1), (1, 0)])


def exchange(value, axes):
    return lax.all_to_all(value, axes, split_axis=0, concat_axis=0, tiled=True)


def split3(value):
    high = value.astype(BF16)
    rest = value - high.astype(F32)
    middle = rest.astype(BF16)
    return high, middle, (rest - middle.astype(F32)).astype(BF16)


def tile_rows(emb_i, i):
    base = 4 * i
    return jnp.concatenate(
        [
            jnp.concatenate([emb_i[base], emb_i[base + 1]], axis=1),
            jnp.concatenate([emb_i[base + 2], emb_i[base + 3]], axis=1),
        ],
        axis=0,
    )


def tile_kernel(
    factors, partner, columns, emb_i, emb_t, out_i, out_t, out_s, acc, sums
):
    scale, shift = factors[0], factors[1]
    high, half = emb_i.shape[1], emb_i.shape[2]
    place = lax.broadcasted_iota(jnp.int32, (2 * high, 1), 0)
    weight = jnp.where(place < high, factors[2], factors[3])
    nt = (((1,), (1,)), ((), ()))
    tn = (((0,), (0,)), ((), ()))

    def grads(similar, i):
        logits = scale * similar + shift
        pair = partner[2 * high * i : 2 * high * (i + 1)] == columns[...]
        signed = jnp.where(pair, -logits, logits)
        small = jnp.exp(-jnp.abs(signed))
        total = 1.0 + small
        inverse = 1.0 / total
        sigmoid = jnp.where(signed >= 0, inverse, small * inverse)
        soft = jnp.maximum(signed, 0.0) + jnp.log(total) + (small - (total - 1.0)) * inverse
        grad = jnp.where(pair, -sigmoid, sigmoid) * weight
        parts = [
            jnp.sum(soft * weight, axis=0, keepdims=True),
            jnp.sum(grad * similar, axis=0, keepdims=True),
            jnp.sum(grad, axis=0, keepdims=True),
        ]
        for j, part in enumerate(parts):
            if i == 0:
                sums[j : j + 1] = part
            else:
                sums[j : j + 1] += part
        return grad.astype(BF16)

    def finish_rows(rounded, rows, i):
        update = lax.dot_general(rounded, rows, tn, preferred_element_type=F32)
        if i == 0:
            acc[...] = update
        else:
            acc[...] += update
        grad_rows = jnp.dot(rounded, emb_t[...], preferred_element_type=F32)
        wide = rows.astype(F32)
        inner = jnp.sum(wide * grad_rows, axis=1, keepdims=True)
        result = (scale * (grad_rows - wide * inner)).astype(BF16)
        out_i[4 * i] = result[:high, :half]
        out_i[4 * i + 1] = result[:high, half:]
        out_i[4 * i + 2] = result[high:, :half]
        out_i[4 * i + 3] = result[high:, half:]

    rows = tile_rows(emb_i, 0)
    similar = lax.dot_general(rows, emb_t[...], nt, preferred_element_type=F32)
    for i in range(4):
        if i < 3:
            later = tile_rows(emb_i, i + 1)
            ahead = lax.dot_general(later, emb_t[...], nt, preferred_element_type=F32)
        rounded = grads(similar, i)
        finish_rows(rounded, rows, i)
        if i < 3:
            rows, similar = later, ahead
    sums[3:] = jnp.zeros_like(sums[3:])
    texts = emb_t[...].astype(F32)
    grads_t = acc[...]
    inner = jnp.sum(texts * grads_t, axis=1, keepdims=True)
    out_t[...] = (scale * (grads_t - texts * inner)).astype(BF16)
    out_s[...] = jnp.broadcast_to(jnp.sum(sums[...], axis=1, keepdims=True), out_s.shape)


def tile_grads(factors, partner, columns, emb_i, emb_t):
    count, width = emb_t.shape
    whole = pl.BlockSpec(memory_space=pltpu.VMEM)
    return pl.pallas_call(
        tile_kernel,
        in_specs=[pl.BlockSpec(memory_space=pltpu.SMEM)] + [whole] * 4,
        out_specs=[whole] * 3,
        out_shape=[
            jax.ShapeDtypeStruct(emb_i.shape, BF16),
            jax.ShapeDtypeStruct(emb_t.shape, BF16),
            jax.ShapeDtypeStruct((8, 128), F32),
        ],
        scratch_shapes=[pltpu.VMEM((count, width), F32), pltpu.VMEM((8, count), F32)],
        compiler_params=pltpu.CompilerParams(vmem_limit_bytes=40 * 1024 * 1024),
    )(factors, partner, columns, emb_i, emb_t)


def half_place(half, j):
    return TEXT_Z + j if half else TEXT_Z - 1 - j


def turn(k):
    return [
        (half_place(half, j), half_place(half, (j + k) % TEXT_Z))
        for half in range(2)
        for j in range(TEXT_Z)
    ]


def finish_kernel(places, first, second, third, fourth, out_i, out_t, out_g, rows):
    image_rows = rows.shape[0] // 16
    text_rows = out_t.shape[0] // 64
    padded = first.shape[1] - text_rows
    for k, piece in enumerate((first, second, third, fourth)):
        place = places[k]
        for s in range(16):
            values = piece[s].astype(F32)
            rows[s * image_rows : (s + 1) * image_rows] = values[:image_rows]
            start = pl.multiple_of(place * (16 * text_rows) + s * text_rows, 8)
            out_t[pl.ds(start, text_rows)] = values[padded:]
            tail = values[image_rows:padded]
            out_g[place, s : s + 1] = tail[0:1] + tail[1:2] + tail[2:3]
        start = pl.multiple_of(place * (16 * image_rows), 8)
        out_i[pl.ds(start, 16 * image_rows)] = rows[...]


def finish(places, pieces, image_total, text_total):
    cols = pieces[0].shape[2]
    whole = pl.BlockSpec(memory_space=pltpu.VMEM)
    return pl.pallas_call(
        finish_kernel,
        in_specs=[pl.BlockSpec(memory_space=pltpu.SMEM)] + [whole] * 4,
        out_specs=[whole] * 3,
        out_shape=[
            jax.ShapeDtypeStruct((image_total, cols), F32),
            jax.ShapeDtypeStruct((text_total, cols), F32),
            jax.ShapeDtypeStruct((4, 16, cols), F32),
        ],
        scratch_shapes=[pltpu.VMEM((image_total // 4, cols), F32)],
        compiler_params=pltpu.CompilerParams(vmem_limit_bytes=24 * 1024 * 1024),
    )(places, *pieces)


def ring(k):
    return [(i, (i + k) % 4) for i in range(4)]


def y_move(value, k):
    return lax.ppermute(value, ("yl", "yh"), [(i, i ^ k) for i in range(4)])


def pick(value, index, axis=0):
    return lax.dynamic_index_in_dim(value, index, axis, keepdims=False)


def local(
    img_feats, txt_feats, img_gain, txt_gain, img_weight, txt_weight, log_scale, bias, pair_perm
):
    yl, z, x = lax.axis_index("yl"), lax.axis_index("z"), lax.axis_index("x")
    yh, core = lax.axis_index("yh"), lax.axis_index("co")
    pair_count = pair_perm.shape[0]
    img_count, txt_count = img_feats.shape[0], txt_feats.shape[0]
    img_half, txt_half = img_count // 2, txt_count // 2
    piece = txt_half // 4
    is_text = (yl == 1) & (z >= TEXT_Z)
    near = jnp.where(z >= TEXT_Z, z - TEXT_Z, TEXT_Z - 1 - z)
    sources = [jnp.mod(x - k + 4, 4) for k in range(4)]
    targets = [jnp.mod(x + k, 4) for k in range(4)]

    image_hidden = hidden_rows(img_feats, img_gain)
    image_hidden, text_gain = lax.optimization_barrier((image_hidden, txt_gain))
    text_hidden = hidden_rows(txt_feats, text_gain)
    share_cols = image_hidden.shape[1] // 4
    parts = jnp.stack(
        [image_hidden[:, i * share_cols : (i + 1) * share_cols] for i in range(4)]
    )
    hidden_x = [pick(parts, x)]
    hidden_x += [lax.ppermute(pick(parts, targets[k]), "x", ring(k)) for k in range(1, 4)]

    text_proj = jnp.dot(text_hidden, txt_weight, preferred_element_type=F32)
    image_proj = jnp.dot(image_hidden, img_weight, preferred_element_type=F32)
    squares = jnp.concatenate(
        [jnp.sum(text_proj * text_proj, axis=1), jnp.sum(image_proj * image_proj, axis=1)]
    )
    squares = squares + swap(squares, "co")
    squares = squares + swap(squares, "yh")
    norms = jnp.sqrt(squares + EPS)[:, None]
    text_norm, image_norm = norms[:txt_count], norms[txt_count:]
    text_emb = (text_proj / text_norm).astype(BF16)
    image_emb = (image_proj / image_norm).astype(BF16)

    def halves(index):
        return jnp.concatenate(
            [
                lax.dynamic_slice_in_dim(image_emb, index * img_half, img_half, 0),
                lax.dynamic_slice_in_dim(text_emb, index * txt_half, txt_half, 0),
            ],
            axis=0,
        )

    kept = halves(core)
    taken = swap(halves(1 - core), "co")
    both = jnp.where(
        core == 0,
        jnp.concatenate([kept, taken], axis=1),
        jnp.concatenate([taken, kept], axis=1),
    )
    width = both.shape[1]
    image_own = both[:img_half]
    text_own = both[img_half:].reshape(4, piece, width)

    got = []
    for k in range(1, 4):
        target = jnp.bitwise_xor(yl * 2 + yh, k)
        got.append(y_move(jnp.concatenate([image_own, pick(text_own, target)], axis=0), k))
    got, hidden_x = lax.optimization_barrier((got, hidden_x))
    slabs = jnp.stack([image_own] + [g[:img_half] for g in got])
    mine = jnp.where(yl == 1, pick(text_own, yl * 2 + yh), got[1][img_half:])
    other = jnp.where(yl == 1, got[0][img_half:], got[2][img_half:])
    chunk = jnp.concatenate([mine, other], axis=1)
    mirror = [(a, Z - 1 - a) for a in range(TEXT_Z, Z)]
    chunk = jnp.where(z >= TEXT_Z, chunk, lax.ppermute(chunk, "z", mirror))
    image_all = [lax.ppermute(slabs, "x", ring(k)) for k in range(1, 4)]
    image_all[0], image_all[2], last = lax.optimization_barrier(
        (image_all[0], image_all[2], chunk)
    )
    image_all = jnp.concatenate([slabs] + image_all)
    chunks = [chunk] + [lax.ppermute(chunk, "z", turn(k)) for k in (1, 2)]
    chunks = jnp.stack([*chunks, lax.ppermute(last, "z", turn(3))])
    text_tile = jnp.stack([chunks, swap(chunks, "co")])
    text_tile = text_tile.reshape(2 * TEXT_Z * piece, 2 * width)

    quarter = yl * 2 + yh
    order = jnp.arange(TEXT_Z, dtype=jnp.int32)
    group = jnp.mod(near - order + TEXT_Z, TEXT_Z) * 4 + x
    columns = (
        group[None, :, None] * txt_count
        + jnp.mod(core + jnp.arange(2, dtype=jnp.int32), 2)[:, None, None] * txt_half
        + quarter * piece
        + jnp.arange(piece, dtype=jnp.int32)[None, None, :]
    ).reshape(1, -1)
    padded = jnp.concatenate([pair_perm, jnp.full((16 * img_count,), -1, jnp.int32)])
    padded = pick(pick(padded.reshape(2, Z, 4, 2, img_half), z, 1), core, 2)
    padded = jnp.where(yl == 0, padded, padded[::-1])
    partner = jnp.stack([pick(padded, source, 1) for source in sources]).reshape(-1, 1)
    logit_scale = jnp.exp(log_scale[0])
    weights = [
        jnp.where((side == 1) & (z >= TEXT_Z), 0.0, 1.0).astype(F32) for side in (yl, 1 - yl)
    ]
    factors = jnp.stack([logit_scale, bias[0], *weights])

    image_part, text_part, part_sums = tile_grads(factors, partner, columns, image_all, text_tile)

    text_part = text_part.reshape(2, TEXT_Z, piece, 2 * width)
    both = text_part[0].astype(F32) + swap(text_part[1], "co").astype(F32)
    rounded = both.astype(BF16)
    image_part = image_part.reshape(4, 4, img_half, width)
    text_got = [lax.ppermute(rounded[k], "z", turn(TEXT_Z - k)) for k in (1, 2)]
    text_got[0], last = lax.optimization_barrier((text_got[0], rounded[3]))
    text_got.append(lax.ppermute(last, "z", turn(1)))
    image_near = [lax.ppermute(image_part[k], "x", ring(-k)) for k in (1, 3)]
    image_far = lax.ppermute(image_part[2], "x", ring(-2))
    text_got, image_near, image_far = lax.optimization_barrier((text_got, image_near, image_far))
    text_sum = both[0]
    for g in text_got:
        text_sum = text_sum + g.astype(F32)
    text_round = text_sum.astype(BF16)
    image_sum = image_part[0].astype(F32)
    for g in (*image_near, image_far):
        image_sum = image_sum + g.astype(F32)

    text_round, image_round = lax.optimization_barrier((text_round, image_sum.astype(BF16)))
    image_sum = image_sum[0]
    for k in range(1, 4):
        image_sum = image_sum + y_move(image_round[k], k).astype(F32)
    text_mirror = lax.ppermute(text_round, "z", [(b, a) for a, b in mirror])
    text_sum, text_mirror, image_sum = lax.optimization_barrier(
        (text_sum, text_mirror, image_sum)
    )
    text_sum = (text_sum + text_mirror.astype(F32)).astype(BF16)
    same, cross = text_sum[:, :width], text_sum[:, width:]
    across, straight, diagonal = [y_move(cross if k & 1 else same, k) for k in range(1, 4)]
    cols = width // 2

    def join_cores(rows):
        kept = lax.dynamic_slice_in_dim(rows, core * cols, cols, 1)
        taken = swap(lax.dynamic_slice_in_dim(rows, (1 - core) * cols, cols, 1), "co")
        return jnp.where(
            core == 0,
            jnp.concatenate([kept, taken], axis=0),
            jnp.concatenate([taken, kept], axis=0),
        )

    image_rows = image_sum / lax.dynamic_slice_in_dim(image_norm, core * img_half, img_half, 0)
    image_du = join_cores(image_rows.astype(BF16))
    straight, image_du = lax.optimization_barrier((straight, image_du))
    du_x = [image_du] + [lax.ppermute(image_du, "x", ring(k)) for k in range(1, 4)]
    transposed = (((0,), (0,)), ((), ()))

    text_rows = jnp.where(
        yh == 0,
        jnp.concatenate([straight, diagonal, same, across], axis=0),
        jnp.concatenate([diagonal, straight, across, same], axis=0),
    )
    text_rows = text_rows.astype(F32) / lax.dynamic_slice_in_dim(
        text_norm, core * txt_half, txt_half, 0
    )
    text_du = join_cores(jnp.where(is_text, text_rows, 0.0).astype(BF16))
    text_weight = lax.dot_general(text_hidden, text_du, transposed, preferred_element_type=F32)
    text_share = text_weight.shape[0] // 4
    text_whole = text_weight
    text_weight = text_weight.reshape(4, text_share, cols)
    got = [
        lax.ppermute(pick(text_weight, targets[k]).astype(BF16), "x", ring(k)) for k in range(1, 4)
    ]
    got[0], du_x = lax.optimization_barrier((got[0], du_x))
    image_weight = lax.dot_general(
        jnp.concatenate(hidden_x), jnp.concatenate(du_x), transposed, preferred_element_type=F32
    )
    img_share, txt_share = share_cols // 16, text_share // 16
    own_weight = lax.dynamic_slice_in_dim(img_weight, x * share_cols, share_cols, 0)
    own_gain = lax.dynamic_slice_in_dim(img_gain, x * share_cols, share_cols, 0)
    small = jnp.concatenate(
        [
            jnp.sum(image_weight * own_weight.astype(F32), axis=1) / own_gain,
            jnp.sum(text_whole * txt_weight.astype(F32), axis=1) / txt_gain,
            part_sums[:3, 0],
        ]
    )
    small = small + swap(small, "co")
    small = small + swap(small, "yh")
    text_weight = pick(text_weight, x)
    for g in got:
        text_weight = text_weight + g.astype(F32)

    slot = 32
    spare = slot - img_share
    used = img_share + 4 * txt_share

    def spare_rows(values):
        rows = jnp.stack(split3(values), axis=1)
        return jnp.pad(rows, ((0, 0), (0, spare - 3), (0, cols - values.shape[1])))

    def joined(blocks):
        rows = blocks[..., img_share:slot, :].astype(F32)
        return rows[..., 0, :] + rows[..., 1, :] + rows[..., 2, :]

    sums = jnp.broadcast_to(small[None, share_cols + 4 * text_share :], (16, 3))
    vector = jnp.concatenate(
        [
            small[:share_cols].reshape(16, img_share),
            small[share_cols : share_cols + 4 * text_share].reshape(16, 4 * txt_share),
            sums,
        ],
        axis=1,
    )
    block = jnp.concatenate(
        [
            image_weight.astype(BF16).reshape(16, img_share, cols),
            spare_rows(vector),
            text_weight.astype(BF16).reshape(16, txt_share, cols),
        ],
        axis=1,
    )
    reduced = exchange(block, ("yl", "z"))
    vector = jnp.sum(joined(reduced), axis=0)
    reduced = jnp.sum(reduced.astype(F32), axis=0)
    ready = jnp.concatenate(
        [
            reduced[:img_share].astype(BF16),
            spare_rows(vector[None, : used + 3])[0],
            reduced[slot:].astype(BF16),
        ],
        axis=0,
    )
    gathered = exchange(jnp.broadcast_to(ready, (16, *ready.shape)), ("yl", "z"))
    pieces = [gathered] + [lax.ppermute(gathered, "x", ring(k)) for k in range(1, 4)]
    image_grad, text_grad, vectors = finish(
        jnp.stack(sources), pieces, img_weight.shape[0], txt_weight.shape[0]
    )
    total = jnp.sum(vectors[:, :, img_share : used + 3], axis=0)
    loss_parts = total[0, 4 * txt_share :]
    return (
        loss_parts[0:1] / pair_count,
        image_grad,
        text_grad,
        vectors[:, :, :img_share].reshape(-1),
        total[:, : 4 * txt_share].reshape(-1),
        loss_parts[1:2] * logit_scale,
        loss_parts[2:3],
    )


def solution(mesh):
    inner = Mesh(mesh.devices.reshape(2, Z, 4, 2, 2), ("yl", "z", "x", "yh", "co"))
    tensor = ("yh", "co")
    return jax.shard_map(
        local,
        mesh=inner,
        in_specs=(
            P(DP, None),
            P(DP, None),
            P(),
            P(),
            P(None, tensor),
            P(None, tensor),
            P(),
            P(),
            P(),
        ),
        out_specs=(P(), P(None, tensor), P(None, tensor), P(), P(), P(), P()),
        check_vma=False,
    )
```
